128 devices in a mesh: seq: 16 (over y_lo, z, core), exp: 8 (over y_hi, x).
Axes of the slice: x: 4, y: 4 (y_hi: 2, y_lo: 2; y = y_hi * 2 + y_lo), z: 4, core: 2. Of those that a mesh axis runs over, the one named last changes fastest.
Arguments:
- queries: bfloat16 [8, 2048, 8192], P('exp', 'seq'), may hold values from -70 to 70
- key_vectors_rows: bfloat16 [8, 2048, 512], P('exp', 'seq'), may hold values from -70 to 70
- values: bfloat16 [8, 2048, 512], P('exp', 'seq'), may hold values from -6 to 6
- expert_tokens: bfloat16 [16384, 4096], P(('seq', 'exp')), may hold values from -6 to 6
- routed_experts: int32 [16384, 8], P(('seq', 'exp')), may hold values from 0 to 127, all different within a row; in each aligned block of 128 rows (0 to 127, 128 to 255, ...) at most 9 rows name the same one
- gate_weights: float32 [16384, 8], P(('seq', 'exp')), may hold values from 0.05 to 0.25
- gate_up_weight: bfloat16 [128, 4096, 1536], P(('seq', 'exp')), may hold values from -0.09375 to 0.09375
- down_weight: bfloat16 [128, 768, 4096], P(('seq', 'exp')), may hold values from -0.21875 to 0.21875
Outputs:
- attention_out: bfloat16 [8, 2048, 8192], P('exp', 'seq')
- expert_out: bfloat16 [16384, 4096], P(('seq', 'exp'))
The draws below stay inside these ranges and needn't reach their ends.
Inputs may be any that keep to these rules, and one draw needn't show every extreme that they name: `routed_experts`: in each aligned block of 128 rows (the rows of one device) no expert is named by more than 9 entries, a bound that some block reaches; a row names 8 different experts.
All inputs are finite; a program needn't handle non-finite values.
Results may differ from the reference program's by a relative error of at most 0.011.
Values may be sent and summed in bfloat16 or wider, within the bound.
No kernel may reach another device: no remote copies, remote signals or barrier semaphores. Data moves between devices by JAX's collectives and lax.ppermute only.
A program may use at most 256 MiB of HBM per device.

```python
import math
import jax
import jax.numpy as jnp
import numpy as np
from jax import lax

D = 4096
QUERY_HEADS = 64
KEY_VALUE_HEADS = 4
HEAD_SIZE = 128
HID = 768
TOP = 8
ROWS_B = 128
SEQUENCE_LENGTH = 2048
ATTENTION_SEQS = 8
EXPERTS = 128
TOK_B = 16384
CAP = 9
BLOCKQ = 512
N_SEQ = 16
N_EXP = 8


def shared_keys(key):
    array_shape = (ATTENTION_SEQS, SEQUENCE_LENGTH, KEY_VALUE_HEADS * HEAD_SIZE)
    normal_part = jnp.clip(jax.random.normal(key, array_shape, jnp.float32), -6.0, 6.0)
    base = normal_part
    return base


def draw_key_vectors_rows(key, part):
    result = shared_keys(key)
    return result.astype(jnp.bfloat16)


def draw_queries(key, part):
    key = jax.random.fold_in(key, 7)
    array_shape = (ATTENTION_SEQS, SEQUENCE_LENGTH, QUERY_HEADS, HEAD_SIZE)
    normal_part = jnp.clip(jax.random.normal(key, array_shape, jnp.float32), -6.0, 6.0)
    base = normal_part
    result = base
    return result.reshape(ATTENTION_SEQS, SEQUENCE_LENGTH, QUERY_HEADS * HEAD_SIZE).astype(jnp.bfloat16)


def shard_levels(key, shape, cuts, least, high):
    factor_of = 1.0
    for axis_at, blocks in cuts:
        heights = jax.random.uniform(jax.random.fold_in(jax.random.fold_in(key, 6), axis_at), (blocks,), jnp.float32, least / len(cuts), high / len(cuts))
        factor_of = factor_of * jnp.repeat(jnp.exp(heights), shape[axis_at] // blocks).reshape((-1,) + (1,) * (len(shape) - 1 - axis_at))
    return factor_of


def deal_out(key, own, number, rows, amount, top, most, skew):
    ranking = jax.random.permutation(key, amount)
    packed, usual = shares(amount, rows * top, most, skew, True), shares(amount, rows * top, most, skew, False)
    places = jnp.arange(amount)

    def named(sizes, turn):
        used = int((sizes > 0).sum())
        fixed = max(1, used // 4)
        passed = fixed + (places - fixed + turn * (used - fixed)) % max(1, amount - fixed)
        return jnp.zeros((amount,), jnp.int32).at[ranking[jnp.where(places < fixed, places, passed)]].set(jnp.asarray(sizes, jnp.int32))

    sizes = jnp.where(number % 4 == 0, named(packed, number // 4), named(usual, number - number // 4 - 1))
    mixed = jax.random.permutation(jax.random.fold_in(own, 3), amount)
    source_of, receiver = mixed[0:amount // 2 * 2:2], mixed[1:amount // 2 * 2:2]
    room = jnp.minimum(sizes[source_of] - 1, most - sizes[receiver]) // 2
    room = jnp.where((source_of == ranking[0]) | (receiver == ranking[0]) | (sizes[receiver] == 0), 0, jnp.maximum(room, 0))
    passed = jax.random.randint(jax.random.fold_in(own, 4), (amount // 2,), 0, 1 << 20) % (room + 1)
    sizes = sizes.at[source_of].add(-passed).at[receiver].add(passed)
    items = jnp.searchsorted(jnp.cumsum(sizes), jnp.arange(rows * top), side="right").astype(jnp.int32)
    grid = items.reshape(top, rows).T
    grid = grid[jax.random.permutation(jax.random.fold_in(own, 1), rows)]
    turn = jax.random.randint(jax.random.fold_in(own, 2), (rows, 1), 0, top)
    return jnp.take_along_axis(grid, (jnp.arange(top)[None, :] + turn) % top, axis=1)


def shares(number_of, total, bound, slope, full):
    loads = [(1 << 20) // math.isqrt(standing ** slope) + 1 for standing in range(1, number_of + 1)]
    largest = bound if full else min(bound, max(-(-total // number_of), total * loads[0] // sum(loads)))
    least = 1 if total - largest >= number_of - 1 else 0
    given, spare = [largest] + [least] * (number_of - 1), total - largest - least * (number_of - 1)
    while spare > 0:
        candidates = [i for i in range(1, number_of) if given[i] < largest] or [i for i in range(1, number_of) if given[i] < bound]
        pool, budget = sum([loads[i] for i in candidates]), spare
        for i in candidates:
            more = min(bound - given[i], max(1, budget * loads[i] // pool), spare)
            given[i] = given[i] + more
            spare = spare - more
    return np.array(given)


def normal_values(stream_key, shape, deviation, limit, cuts=(), kind=jnp.bfloat16):
    values = deviation * jax.random.normal(stream_key, shape, jnp.float32)
    if cuts:
        values = values * shard_levels(stream_key, shape, cuts, -0.22, 0.18)
    return jnp.clip(values, -limit, limit).astype(kind)


def setup_inputs(seed: int = 0) -> dict:
    seeds = jax.random.split(jax.random.key(seed), 9)
    queries = draw_queries(jax.random.fold_in(seeds[8], 71), 0)
    key_vectors_rows = draw_key_vectors_rows(jax.random.fold_in(seeds[8], 71), 0)
    values = normal_values(seeds[2], (ATTENTION_SEQS, SEQUENCE_LENGTH, KEY_VALUE_HEADS * HEAD_SIZE), 1.0, 6.0, ((0, 8), (1, 16)))
    expert_tokens = normal_values(seeds[3], (TOK_B, D), 1.0, 6.0, ((0, 128),))
    routed_experts_keys = jax.random.split(jax.random.fold_in(seeds[4], 1), TOK_B // ROWS_B)
    routed_experts_turns = jax.random.permutation(jax.random.fold_in(seeds[4], 3), TOK_B // ROWS_B)
    routed_experts = jax.vmap(lambda own, number: deal_out(jax.random.fold_in(seeds[4], 2), own, number, ROWS_B, EXPERTS, TOP, CAP, 2))(routed_experts_keys, routed_experts_turns).reshape((TOK_B, TOP))
    gate_weights = jnp.clip(0.05 + 0.2 * jax.random.uniform(seeds[5], (TOK_B, TOP), jnp.float32) ** shard_levels(seeds[5], (TOK_B, TOP), ((0, 128),), -0.2, 0.2), 0.05, 0.25)
    gate_up_weight = normal_values(seeds[6], (EXPERTS, D, 2 * HID), D ** -0.5, 0.09375, ((0, 128),))
    down_weight = normal_values(seeds[7], (EXPERTS, HID, D), HID ** -0.5, 0.21875, ((0, 128),))
    return {"queries": queries, "key_vectors_rows": key_vectors_rows, "values": values, "expert_tokens": expert_tokens, "routed_experts": routed_experts, "gate_weights": gate_weights, "gate_up_weight": gate_up_weight, "down_weight": down_weight}


def attend(query_group, key_head, value_head, block_size):
    length = query_group.shape[0]
    scale = query_group.shape[2] ** -0.5
    pieces = []
    for block_index in range(length // block_size):
        finish = (block_index + 1) * block_size
        query_block = query_group[block_index * block_size:finish]
        scores = jnp.einsum("qhd,kd->hqk", query_block.astype(jnp.float32), key_head[:finish].astype(jnp.float32)) * scale
        query_pos = block_index * block_size + jnp.arange(block_size, dtype=jnp.int32)
        key_pos = jnp.arange(finish, dtype=jnp.int32)
        scores = jnp.where(key_pos[None, None, :] <= query_pos[None, :, None], scores, -jnp.inf)
        maximum = jnp.max(scores, axis=-1, keepdims=True)
        numerators = jnp.exp(scores - maximum)
        totals = jnp.sum(numerators, axis=-1, keepdims=True)
        weights = (numerators / totals).astype(jnp.bfloat16)
        mixed_rows = jnp.einsum("hqk,kd->qhd", weights.astype(jnp.float32), value_head[:finish].astype(jnp.float32))
        pieces.append(mixed_rows.astype(jnp.bfloat16))
    return jnp.concatenate(pieces, axis=0)


def reference(queries, key_vectors_rows, values, expert_tokens, routed_experts, gate_weights, gate_up_weight, down_weight):
    query_group_width = QUERY_HEADS // KEY_VALUE_HEADS
    attention_list = []
    for sequence_index in range(ATTENTION_SEQS):
        heads_of_queries = queries[sequence_index].reshape(SEQUENCE_LENGTH, KEY_VALUE_HEADS, query_group_width, HEAD_SIZE).transpose(1, 0, 2, 3)
        heads_of_keys = key_vectors_rows[sequence_index].reshape(SEQUENCE_LENGTH, KEY_VALUE_HEADS, HEAD_SIZE).transpose(1, 0, 2)
        heads_of_values = values[sequence_index].reshape(SEQUENCE_LENGTH, KEY_VALUE_HEADS, HEAD_SIZE).transpose(1, 0, 2)

        def one_group(triple):
            return attend(triple[0], triple[1], triple[2], BLOCKQ)

        result = lax.map(one_group, (heads_of_queries, heads_of_keys, heads_of_values))
        attention_list.append(result.transpose(1, 0, 2, 3).reshape(SEQUENCE_LENGTH, QUERY_HEADS * HEAD_SIZE))
    attention_out = jnp.stack(attention_list)

    sources = N_SEQ * N_EXP
    per_block = ROWS_B * TOP
    flat_ids = routed_experts.reshape(sources, per_block)
    onehot = (flat_ids[:, :, None] == jnp.arange(EXPERTS, dtype=jnp.int32)[None, None, :]).astype(jnp.int32)
    running = jnp.cumsum(onehot, axis=1)
    slot_index = jnp.sum(onehot * running, axis=2) - 1
    places = (jnp.arange(sources, dtype=jnp.int32)[:, None] * CAP + slot_index).reshape(-1).astype(jnp.int32)
    token_index = (jnp.arange(TOK_B * TOP, dtype=jnp.int32) // TOP).astype(jnp.int32)
    flat_experts = routed_experts.reshape(-1)
    slot_table = jnp.full((EXPERTS, sources * CAP), TOK_B, jnp.int32).at[flat_experts, places].set(token_index)
    scales = jnp.zeros((EXPERTS, sources * CAP), jnp.float32).at[flat_experts, places].set(gate_weights.reshape(-1))
    padded = jnp.concatenate([expert_tokens, jnp.zeros((1, D), jnp.bfloat16)], axis=0)

    def one_expert(totals, inputs):
        gate_up_matrix, down_matrix, rows_index, row_scales = inputs
        gathered = padded[rows_index]
        projected = jnp.dot(gathered, gate_up_matrix, preferred_element_type=jnp.float32)
        hidden = (jax.nn.silu(projected[:, :HID]) * projected[:, HID:]).astype(jnp.bfloat16)
        produced = jnp.dot(hidden, down_matrix, preferred_element_type=jnp.float32).astype(jnp.bfloat16)
        totals = totals.at[rows_index].add(row_scales[:, None] * produced.astype(jnp.float32))
        return totals, None

    totals, unused = lax.scan(one_expert, jnp.zeros((TOK_B + 1, D), jnp.float32), (gate_up_weight, down_weight, slot_table, scales))
    expert_out = totals[:TOK_B].astype(jnp.bfloat16)
    return (attention_out, expert_out)
```

```python
import functools

import jax
import jax.numpy as jnp
from jax import lax
from jax.experimental import pallas as pl
from jax.experimental.pallas import tpu as pltpu
from jax.sharding import PartitionSpec as P

HEAD_SIZE = 128
BAND = 8
FOLD = 512
BF = jnp.bfloat16
F32 = jnp.float32
VMEM = 56 * 1024 * 1024


def iota(shape, dim):
    return lax.broadcasted_iota(jnp.int32, shape, dim)


def dot(a, b):
    return jnp.dot(a, b, preferred_element_type=F32)


def fold_matrix():
    row, col = iota((256, 256), 0), iota((256, 256), 1)
    return (col == (row & 7) * 32 + (row >> 3)).astype(F32).astype(BF)


def unfold_matrix():
    row, col = iota((256, 256), 0), iota((256, 256), 1)
    return (col == (row & 31) * 8 + (row >> 5)).astype(F32).astype(BF)


def ranks(routed):
    tokens = routed.shape[0]
    experts = iota((tokens, 128), 1)
    named = jnp.zeros((tokens, 128), F32)
    for j in range(routed.shape[1]):
        named = jnp.where(routed[:, j : j + 1] == experts, 1.0, named)
    earlier = (iota((tokens, tokens), 1) < iota((tokens, tokens), 0)).astype(F32).astype(BF)
    before = dot(earlier, named.astype(BF))
    return jnp.where(named > 0.5, before, -1.0)


def dispatch_kernel(routed_ref, tokens_ref, out_ref, rank_ref):
    step = pl.program_id(0)
    width = tokens_ref.shape[1]

    @pl.when(step == 0)
    def _():
        rank_ref[...] = ranks(routed_ref[...]).T

    expand = (iota((256, 128), 1) == step * 32 + (iota((256, 128), 0) >> 3)).astype(F32).astype(BF)
    spread = dot(expand, rank_ref[...].astype(BF))
    slot = (iota((256, 128), 0) & 7).astype(F32)
    ninth = rank_ref[pl.ds(pl.multiple_of(step * 32, 32), 32), :]
    pick = jnp.concatenate(
        [jnp.where(spread == slot, 1.0, 0.0), jnp.where(ninth == float(BAND), 1.0, 0.0)], axis=0
    ).astype(BF)
    folded = []
    for c in range(width // FOLD):
        cols = slice(c * FOLD, (c + 1) * FOLD)
        rows = dot(pick, tokens_ref[:, cols]).astype(BF)
        out_ref[:, cols] = rows[:256]
        folded.append(rows[256:])
    out_ref[:, width:] = dot(fold_matrix(), jnp.concatenate(folded, axis=0)).astype(BF)


def dispatch(routed, tokens):
    width = tokens.shape[1]
    return pl.pallas_call(
        dispatch_kernel,
        grid=(4,),
        in_specs=[
            pl.BlockSpec(routed.shape, lambda i: (0, 0)),
            pl.BlockSpec(tokens.shape, lambda i: (0, 0)),
        ],
        out_specs=pl.BlockSpec((256, width + FOLD), lambda i: (i, 0)),
        out_shape=jax.ShapeDtypeStruct((128 * BAND, width + FOLD), BF),
        scratch_shapes=[pltpu.VMEM((128, 128), F32)],
        compiler_params=pltpu.CompilerParams(vmem_limit_bytes=VMEM),
        cost_estimate=pl.CostEstimate(flops=2 * 1152 * 128 * 4096, bytes_accessed=11_000_000, transcendentals=0),
        name="dispatch_rows",
    )(routed, tokens)


def gates_kernel(routed_ref, gates_ref, out_ref):
    routed = routed_ref[...]
    tokens = routed.shape[0]
    rank = ranks(routed)
    experts = iota((tokens, 128), 1)
    gate = jnp.zeros((tokens, 128), F32)
    for j in range(routed.shape[1]):
        gate = jnp.where(routed[:, j : j + 1] == experts, gates_ref[:, j : j + 1], gate)
    high = gate.astype(BF)
    low = (gate - high.astype(F32)).astype(BF)
    wide = 128 * BAND
    expand = (iota((128, wide), 0) == (iota((128, wide), 1) >> 3)).astype(F32).astype(BF)
    chosen = dot(rank.astype(BF), expand) == (iota((tokens, wide), 1) & 7).astype(F32)
    for part, value in enumerate((high, low)):
        rows = slice(part * tokens, (part + 1) * tokens)
        out_ref[rows, :wide] = jnp.where(chosen, dot(value, expand), 0.0).astype(BF)
        out_ref[rows, wide:] = jnp.where(rank == float(BAND), value.astype(F32), 0.0).astype(BF)


def gate_matrix(routed, gates):
    tokens = routed.shape[0]
    return pl.pallas_call(
        gates_kernel,
        out_shape=jax.ShapeDtypeStruct((2 * tokens, 128 * (BAND + 1)), BF),
        compiler_params=pltpu.CompilerParams(vmem_limit_bytes=VMEM),
        cost_estimate=pl.CostEstimate(flops=6 * 128 * 128 * 1024, bytes_accessed=700_000, transcendentals=0),
        name="gate_matrix",
    )(routed, gates)


def experts_kernel(rows_ref, last_ref, up_ref, down_ref, out_ref, ninth_ref, sum_ref, hidden_ref, tail_ref, *, depth_steps):
    step = pl.program_id(0)
    depth = rows_ref.shape[1]
    units = down_ref.shape[0]

    @pl.when(step == 0)
    def _():
        unfold = unfold_matrix()
        for b in range(4):
            piece = dot(unfold, last_ref[b * 256 : (b + 1) * 256, :]).astype(BF)
            for r in range(8):
                at = r * FOLD
                ninth_ref[at // depth, b * 32 : (b + 1) * 32, at % depth : at % depth + FOLD] = piece[
                    r * 32 : (r + 1) * 32
                ]

    @pl.when(step < depth_steps)
    def _():
        rows = jnp.concatenate([rows_ref[...], ninth_ref[step]], axis=0)
        part = dot(rows, up_ref[...])

        @pl.when(step == 0)
        def _():
            sum_ref[...] = part

        @pl.when(step > 0)
        def _():
            sum_ref[...] += part

    @pl.when(step == depth_steps)
    def _():
        gate = sum_ref[:, :units]
        hidden_ref[...] = (gate / (1.0 + jnp.exp(-gate)) * sum_ref[:, units:]).astype(BF)

    @pl.when((step >= depth_steps) & (step < depth_steps + 8))
    def _():
        made = dot(hidden_ref[...], down_ref[...]).astype(BF)
        out_ref[...] = made[:1024]
        tail_ref[step - depth_steps] = made[1024:]

    @pl.when(step == depth_steps + 8)
    def _():
        fold = fold_matrix()
        for b in range(4):
            piece = jnp.concatenate([tail_ref[r, b * 32 : (b + 1) * 32, :] for r in range(8)], axis=0)
            out_ref[b * 256 : (b + 1) * 256, :] = dot(fold, piece).astype(BF)


def run_experts(arrived, up, down, depth=1024):
    rows = arrived.shape[0]
    width = up.shape[1]
    units = down.shape[1]
    depth_steps = width // depth
    all_rows = rows + 128
    return pl.pallas_call(
        functools.partial(experts_kernel, depth_steps=depth_steps),
        grid=(depth_steps + 9,),
        in_specs=[
            pl.BlockSpec((rows, depth), lambda i: (0, jnp.minimum(i, depth_steps - 1))),
            pl.BlockSpec((rows, FOLD), lambda i: (0, width // FOLD)),
            pl.BlockSpec((None, depth, 2 * units), lambda i: (0, jnp.minimum(i, depth_steps - 1), 0)),
            pl.BlockSpec((None, units, FOLD), lambda i: (0, 0, jnp.clip(i - depth_steps, 0, 7))),
        ],
        out_specs=pl.BlockSpec((rows, FOLD), lambda i: (0, jnp.clip(i - depth_steps, 0, 8))),
        out_shape=jax.ShapeDtypeStruct(arrived.shape, BF),
        scratch_shapes=[
            pltpu.VMEM((depth_steps, 128, depth), BF),
            pltpu.VMEM((all_rows, 2 * units), F32),
            pltpu.VMEM((all_rows, units), BF),
            pltpu.VMEM((8, 128, FOLD), BF),
        ],
        compiler_params=pltpu.CompilerParams(vmem_limit_bytes=VMEM),
        cost_estimate=pl.CostEstimate(
            flops=2 * all_rows * units * 3 * width, bytes_accessed=38_000_000, transcendentals=all_rows * units
        ),
        name="run_experts",
    )(arrived, arrived, up, down)


def combine_kernel(gates_ref, rows_ref, last_ref, out_ref, ninth_ref):
    step = pl.program_id(0)
    tokens = out_ref.shape[0]
    wide = rows_ref.shape[0]

    @pl.when(step == 0)
    def _():
        unfold = unfold_matrix()
        for b in range(4):
            piece = dot(unfold, last_ref[b * 256 : (b + 1) * 256, :]).astype(BF)
            for r in range(8):
                ninth_ref[r, b * 32 : (b + 1) * 32, :] = piece[r * 32 : (r + 1) * 32]

    both = dot(gates_ref[:, :wide], rows_ref[...]) + dot(gates_ref[:, wide:], ninth_ref[step])
    out_ref[...] = (both[:tokens] + both[tokens:]).astype(BF)


def combine(gates, returned):
    rows = returned.shape[0]
    width = returned.shape[1] - FOLD
    tokens = gates.shape[0] // 2
    return pl.pallas_call(
        combine_kernel,
        grid=(width // FOLD,),
        in_specs=[
            pl.BlockSpec(gates.shape, lambda i: (0, 0)),
            pl.BlockSpec((rows, FOLD), lambda i: (0, i)),
            pl.BlockSpec((rows, FOLD), lambda i: (0, width // FOLD)),
        ],
        out_specs=pl.BlockSpec((tokens, FOLD), lambda i: (0, i)),
        out_shape=jax.ShapeDtypeStruct((tokens, width), BF),
        scratch_shapes=[pltpu.VMEM((8, 128, FOLD), BF)],
        compiler_params=pltpu.CompilerParams(vmem_limit_bytes=VMEM),
        cost_estimate=pl.CostEstimate(flops=2 * 256 * 1152 * 4096, bytes_accessed=11_000_000, transcendentals=0),
        name="combine_rows",
    )(gates, returned, returned)


def attention_kernel(first_ref, queries_ref, keys_ref, values_ref, out_ref):
    rows = queries_ref.shape[0]
    length = keys_ref.shape[0]
    heads = queries_ref.shape[1] // HEAD_SIZE
    position = first_ref[0] + iota((rows, length), 0)
    seen = iota((rows, length), 1) <= position
    factor = HEAD_SIZE**-0.5 * 1.4426950408889634
    for h in range(heads):
        cols = slice(h * HEAD_SIZE, (h + 1) * HEAD_SIZE)
        scores = lax.dot_general(
            queries_ref[:, cols], keys_ref[...], (((1,), (1,)), ((), ())), preferred_element_type=F32
        )
        scores = jnp.where(seen, scores, -1e30)
        top = jnp.max(scores, axis=-1, keepdims=True)
        part = jnp.exp2((scores - top) * factor)
        total = jnp.sum(part, axis=-1, keepdims=True)
        mixed = dot(part.astype(BF), values_ref[...])
        out_ref[:, cols] = (mixed / total).astype(BF)


def attention(first, queries, pairs, heads_per_step=4):
    rows, width = queries.shape
    length = pairs.shape[0]
    kv_heads = pairs.shape[1] // (2 * HEAD_SIZE)
    steps = width // (heads_per_step * HEAD_SIZE)
    per_kv = steps // kv_heads
    block = (rows, heads_per_step * HEAD_SIZE)
    return pl.pallas_call(
        attention_kernel,
        grid=(steps,),
        in_specs=[
            pl.BlockSpec(memory_space=pltpu.SMEM),
            pl.BlockSpec(block, lambda i: (0, i)),
            pl.BlockSpec((length, HEAD_SIZE), lambda i: (0, i // per_kv)),
            pl.BlockSpec((length, HEAD_SIZE), lambda i: (0, kv_heads + i // per_kv)),
        ],
        out_specs=pl.BlockSpec(block, lambda i: (0, i)),
        out_shape=jax.ShapeDtypeStruct(queries.shape, BF),
        compiler_params=pltpu.CompilerParams(vmem_limit_bytes=VMEM),
        cost_estimate=pl.CostEstimate(
            flops=4 * rows * width * length, bytes_accessed=9_000_000, transcendentals=rows * length * width // HEAD_SIZE
        ),
        name="attention_rows",
    )(first, queries, pairs, pairs)


def on_device(queries, keys, values, tokens, routed, gates, up, down):
    pairs = jnp.concatenate([keys[0], values[0]], axis=1)
    pairs = lax.all_gather(pairs, "seq", axis=0, tiled=True)
    everywhere = ("seq", "exp")
    outgoing = dispatch(routed, tokens)
    arrived = lax.all_to_all(outgoing, everywhere, split_axis=0, concat_axis=0, tiled=True)
    weights = gate_matrix(routed, gates)
    made = run_experts(arrived, up, down)
    made, own = lax.optimization_barrier((made, queries[0]))
    returned = lax.all_to_all(made, everywhere, split_axis=0, concat_axis=0, tiled=True)
    first = (lax.axis_index("seq") * own.shape[0]).astype(jnp.int32).reshape(1)
    attended = attention(first, own, pairs)
    return (attended[None], combine(weights, returned))


def solution(mesh):
    spread = P(("seq", "exp"), None)
    in_specs = (P("exp", "seq", None),) * 3 + (spread,) * 3 + (P(("seq", "exp"), None, None),) * 2
    out_specs = (P("exp", "seq", None), spread)
    return jax.shard_map(on_device, mesh=mesh, in_specs=in_specs, out_specs=out_specs, check_vma=False)
```

```python
import functools

import jax
import jax.numpy as jnp
from jax import lax
from jax.experimental import pallas as pl
from jax.experimental.pallas import tpu as pltpu
from jax.sharding import PartitionSpec as P

HEAD_SIZE = 128
BAND = 8
FOLD = 512
BF = jnp.bfloat16
F32 = jnp.float32
VMEM = 56 * 1024 * 1024


def iota(shape, dim):
    return lax.broadcasted_iota(jnp.int32, shape, dim)


def dot(a, b):
    return jnp.dot(a, b, preferred_element_type=F32)


def fold_matrix():
    row, col = iota((256, 256), 0), iota((256, 256), 1)
    return (col == (row & 7) * 32 + (row >> 3)).astype(F32).astype(BF)


def unfold_matrix():
    row, col = iota((256, 256), 0), iota((256, 256), 1)
    return (col == (row & 31) * 8 + (row >> 5)).astype(F32).astype(BF)


def ranks(routed):
    tokens = routed.shape[1]
    experts = iota((128, tokens), 0)
    named = jnp.zeros((128, tokens), F32)
    for j in range(routed.shape[0]):
        named = jnp.where(routed[j : j + 1, :] == experts, 1.0, named)
    earlier = (iota((tokens, tokens), 0) < iota((tokens, tokens), 1)).astype(F32).astype(BF)
    before = dot(named.astype(BF), earlier)
    return jnp.where(named > 0.5, before, -1.0)


def send_block(rows_ref, fold_ref, out_hbm, sems, b):
    width = rows_ref.shape[1]
    rows = pl.ds(b * 256, 256)
    copies = [
        pltpu.make_async_copy(
            rows_ref.at[pl.ds(b * 288, 256), :], out_hbm.at[rows, pl.ds(0, width)], sems.at[b, 0]
        ),
        pltpu.make_async_copy(fold_ref.at[rows, :], out_hbm.at[rows, pl.ds(width, FOLD)], sems.at[b, 1]),
    ]
    copies[0].start()
    ninth = slice(b * 288 + 256, (b + 1) * 288)
    piece = jnp.concatenate([rows_ref[ninth, r * FOLD : (r + 1) * FOLD] for r in range(8)], axis=0)
    fold_ref[b * 256 : (b + 1) * 256, :] = dot(fold_matrix(), piece).astype(BF)
    copies[1].start()
    return copies


def dispatch_kernel(routed_ref, tokens_hbm, out_hbm, tokens_ref, rows_ref, fold_ref, in_sem, sems):
    width = tokens_ref.shape[1]
    load = pltpu.make_async_copy(tokens_hbm, tokens_ref, in_sem.at[0])
    load.start()
    rank = ranks(routed_ref[...])
    low = rank.astype(BF)
    copies = []
    for b in range(4):
        expand = (iota((256, 128), 1) == b * 32 + (iota((256, 128), 0) >> 3)).astype(F32).astype(BF)
        band = dot(expand, low) == (iota((256, 128), 0) & 7).astype(F32)
        ninth = rank[b * 32 : (b + 1) * 32] == float(BAND)
        pick = jnp.concatenate([jnp.where(band, 1.0, 0.0), jnp.where(ninth, 1.0, 0.0)], axis=0).astype(BF)
        if b == 0:
            load.wait()
        for c in range(width // FOLD):
            cols = slice(c * FOLD, (c + 1) * FOLD)
            rows_ref[b * 288 : (b + 1) * 288, cols] = dot(pick, tokens_ref[:, cols]).astype(BF)
        copies += send_block(rows_ref, fold_ref, out_hbm, sems, b)
    for copy in copies:
        copy.wait()


def dispatch(routed, tokens):
    width = tokens.shape[1]
    return pl.pallas_call(
        dispatch_kernel,
        in_specs=[pl.BlockSpec(memory_space=pltpu.VMEM), pl.BlockSpec(memory_space=pl.ANY)],
        out_specs=pl.BlockSpec(memory_space=pl.ANY),
        out_shape=jax.ShapeDtypeStruct((128 * BAND, width + FOLD), BF),
        scratch_shapes=[
            pltpu.VMEM(tokens.shape, BF),
            pltpu.VMEM((4 * 288, width), BF),
            pltpu.VMEM((1024, FOLD), BF),
            pltpu.SemaphoreType.DMA((1,)),
            pltpu.SemaphoreType.DMA((4, 2)),
        ],
        compiler_params=pltpu.CompilerParams(vmem_limit_bytes=VMEM),
        cost_estimate=pl.CostEstimate(flops=2 * 1152 * 128 * 4096, bytes_accessed=11_000_000, transcendentals=0),
        name="dispatch_rows",
    )(routed, tokens)


def gates_kernel(routed_ref, gates_ref, out_ref):
    routed = routed_ref[...]
    tokens = routed.shape[1]
    rank = ranks(routed)
    experts = iota((128, tokens), 0)
    gate = jnp.zeros((128, tokens), F32)
    for j in range(routed.shape[0]):
        gate = jnp.where(routed[j : j + 1, :] == experts, gates_ref[j : j + 1, :], gate)
    gate = gate.T
    rank = rank.T
    high = gate.astype(BF)
    low = (gate - high.astype(F32)).astype(BF)
    wide = 128 * BAND
    expand = (iota((128, wide), 0) == (iota((128, wide), 1) >> 3)).astype(F32).astype(BF)
    chosen = dot(rank.astype(BF), expand) == (iota((tokens, wide), 1) & 7).astype(F32)
    for part, value in enumerate((high, low)):
        rows = slice(part * tokens, (part + 1) * tokens)
        out_ref[rows, :wide] = jnp.where(chosen, dot(value, expand), 0.0).astype(BF)
        out_ref[rows, wide:] = jnp.where(rank == float(BAND), value.astype(F32), 0.0).astype(BF)


def gate_matrix(routed, gates):
    tokens = routed.shape[1]
    return pl.pallas_call(
        gates_kernel,
        out_shape=jax.ShapeDtypeStruct((2 * tokens, 128 * (BAND + 1)), BF),
        compiler_params=pltpu.CompilerParams(vmem_limit_bytes=VMEM),
        cost_estimate=pl.CostEstimate(flops=6 * 128 * 128 * 1024, bytes_accessed=700_000, transcendentals=0),
        name="gate_matrix",
    )(routed, gates)


def experts_kernel(
    rows_hbm, up_hbm, down_hbm, out_hbm,
    rows_ref, last_ref, up_ref, down_ref, sum_ref, hidden_ref, made_ref, fold_ref,
    row_sems, up_sems, down_sems, sems,
    *, deep, part, wide,
):
    width = rows_ref.shape[1]
    units = hidden_ref.shape[1]
    chunks = width // deep

    def load_rows(b):
        rows = pl.ds(b * 256, 256)
        return [
            pltpu.make_async_copy(rows_hbm.at[rows, pl.ds(width, FOLD)], last_ref.at[rows, :], row_sems.at[b, 0]),
            pltpu.make_async_copy(
                rows_hbm.at[rows, pl.ds(0, width)], rows_ref.at[pl.ds(b * 288, 256), :], row_sems.at[b, 1]
            ),
        ]

    def load_up(k):
        rows = pl.ds(k * deep, deep)
        return pltpu.make_async_copy(up_hbm.at[0, rows, :], up_ref.at[rows, :], up_sems.at[k])

    def load_down(k):
        rows = pl.ds(k * 256, 256)
        return pltpu.make_async_copy(down_hbm.at[0, rows, :], down_ref.at[rows, :], down_sems.at[k])

    row_loads = [load_rows(b) for b in range(4)]
    up_loads = [load_up(k) for k in range(chunks)]
    down_loads = [load_down(k) for k in range(units // 256)]
    later = row_loads[1] + row_loads[2] + row_loads[3] + down_loads
    for load in row_loads[0] + up_loads:
        load.start()

    def ready(b):
        for load in row_loads[b]:
            load.wait()
        piece = dot(unfold_matrix(), last_ref[b * 256 : (b + 1) * 256, :]).astype(BF)
        for r in range(8):
            rows_ref[b * 288 + 256 : (b + 1) * 288, r * FOLD : (r + 1) * FOLD] = piece[r * 32 : (r + 1) * 32]

    def activate(gate, linear):
        return (gate / (1.0 + jnp.exp(-gate)) * linear).astype(BF)

    ready(0)
    for k in range(chunks):
        up_loads[k].wait()
        cols = slice(k * deep, (k + 1) * deep)
        term = dot(rows_ref[:288, cols], up_ref[cols, :])
        if k == 0:
            sum_ref[...] = term
        elif k < chunks - 1:
            sum_ref[...] += term
        else:
            term = sum_ref[...] + term
            hidden_ref[:288, :] = activate(term[:, :units], term[:, units:])
        count = -(-len(later) // chunks)
        for load in later[k * count : (k + 1) * count]:
            load.start()
    for first, last in ((1, 2), (2, 4)):
        for b in range(first, last):
            ready(b)
        rows = slice(first * 288, last * 288)
        for c in range(units // part):
            cols = slice(c * part, (c + 1) * part)
            gate = dot(rows_ref[rows, :], up_ref[:, cols])
            linear = dot(rows_ref[rows, :], up_ref[:, units + c * part : units + (c + 1) * part])
            hidden_ref[rows, cols] = activate(gate, linear)
    for load in down_loads:
        load.wait()
    copies = []
    for first, last in ((0, 2), (2, 4)):
        rows = slice(first * 288, last * 288)
        for c in range(width // wide):
            cols = slice(c * wide, (c + 1) * wide)
            made_ref[rows, cols] = dot(hidden_ref[rows, :], down_ref[:, cols]).astype(BF)
        for b in range(first, last):
            copies += send_block(made_ref, fold_ref, out_hbm, sems, b)
    for copy in copies:
        copy.wait()


def run_experts(arrived, up, down, deep=1024, part=256, wide=512):
    rows = arrived.shape[0]
    width = up.shape[1]
    units = down.shape[1]
    all_rows = rows + 128
    return pl.pallas_call(
        functools.partial(experts_kernel, deep=deep, part=part, wide=wide),
        in_specs=[pl.BlockSpec(memory_space=pl.ANY)] * 3,
        out_specs=pl.BlockSpec(memory_space=pl.ANY),
        out_shape=jax.ShapeDtypeStruct(arrived.shape, BF),
        scratch_shapes=[
            pltpu.VMEM((all_rows, width), BF),
            pltpu.VMEM((rows, FOLD), BF),
            pltpu.VMEM((width, 2 * units), BF),
            pltpu.VMEM((units, width), BF),
            pltpu.VMEM((288, 2 * units), F32),
            pltpu.VMEM((all_rows, units), BF),
            pltpu.VMEM((all_rows, width), BF),
            pltpu.VMEM((rows, FOLD), BF),
            pltpu.SemaphoreType.DMA((4, 2)),
            pltpu.SemaphoreType.DMA((width // deep,)),
            pltpu.SemaphoreType.DMA((units // 256,)),
            pltpu.SemaphoreType.DMA((4, 2)),
        ],
        compiler_params=pltpu.CompilerParams(vmem_limit_bytes=VMEM),
        cost_estimate=pl.CostEstimate(
            flops=2 * all_rows * units * 3 * width, bytes_accessed=38_000_000, transcendentals=all_rows * units
        ),
        name="run_experts",
    )(arrived, up, down)


def combine_kernel(gates_ref, rows_hbm, out_hbm, rows_ref, ninth_ref, sum_ref, out_ref, in_sems, sem):
    tokens, width = out_ref.shape
    wide = rows_ref.shape[0]
    loads = [
        pltpu.make_async_copy(rows_hbm.at[pl.ds(b * 128, 128), :], rows_ref.at[pl.ds(b * 128, 128), :], in_sems.at[b])
        for b in range(wide // 128)
    ]
    for load in loads:
        load.start()
    unfold = unfold_matrix()
    for half in range(2):
        for b in range(half * 4, half * 4 + 4):
            loads[b].wait()
        for b in range(half * 2, half * 2 + 2):
            piece = dot(unfold, rows_ref[b * 256 : (b + 1) * 256, width:]).astype(BF)
            for r in range(8):
                ninth_ref[r, b * 32 : (b + 1) * 32, :] = piece[r * 32 : (r + 1) * 32]
        rows = slice(half * 512, (half + 1) * 512)
        for c in range(width // FOLD):
            cols = slice(c * FOLD, (c + 1) * FOLD)
            both = dot(gates_ref[:, rows], rows_ref[rows, cols])
            if half == 0:
                sum_ref[:, cols] = both[:tokens] + both[tokens:]
            else:
                both += dot(gates_ref[:, wide:], ninth_ref[c])
                out_ref[:, cols] = (sum_ref[:, cols] + both[:tokens] + both[tokens:]).astype(BF)
    copy = pltpu.make_async_copy(out_ref, out_hbm, sem.at[0])
    copy.start()
    copy.wait()


def combine(gates, returned):
    rows = returned.shape[0]
    width = returned.shape[1] - FOLD
    tokens = gates.shape[0] // 2
    return pl.pallas_call(
        combine_kernel,
        in_specs=[pl.BlockSpec(memory_space=pltpu.VMEM), pl.BlockSpec(memory_space=pl.ANY)],
        out_specs=pl.BlockSpec(memory_space=pl.ANY),
        out_shape=jax.ShapeDtypeStruct((tokens, width), BF),
        scratch_shapes=[
            pltpu.VMEM(returned.shape, BF),
            pltpu.VMEM((8, 128, FOLD), BF),
            pltpu.VMEM((tokens, width), F32),
            pltpu.VMEM((tokens, width), BF),
            pltpu.SemaphoreType.DMA((rows // 128,)),
            pltpu.SemaphoreType.DMA((1,)),
        ],
        compiler_params=pltpu.CompilerParams(vmem_limit_bytes=VMEM),
        cost_estimate=pl.CostEstimate(flops=2 * 256 * 1152 * 4096, bytes_accessed=11_000_000, transcendentals=0),
        name="combine_rows",
    )(gates, returned)


def attention_kernel(first_ref, queries_ref, keys_ref, values_ref, out_ref):
    rows = queries_ref.shape[0]
    length = keys_ref.shape[0]
    heads = queries_ref.shape[1] // HEAD_SIZE
    position = first_ref[0] + iota((rows, length), 0)
    seen = iota((rows, length), 1) <= position
    factor = HEAD_SIZE**-0.5 * 1.4426950408889634
    for h in range(heads):
        cols = slice(h * HEAD_SIZE, (h + 1) * HEAD_SIZE)
        scores = lax.dot_general(
            queries_ref[:, cols], keys_ref[...], (((1,), (1,)), ((), ())), preferred_element_type=F32
        )
        scores = jnp.where(seen, scores, -1e30)
        top = jnp.max(scores, axis=-1, keepdims=True)
        part = jnp.exp2((scores - top) * factor)
        total = jnp.sum(part, axis=-1, keepdims=True)
        mixed = dot(part.astype(BF), values_ref[...])
        out_ref[:, cols] = (mixed / total).astype(BF)


def attention(first, queries, pairs, heads_per_step=16):
    rows, width = queries.shape
    length = pairs.shape[0]
    kv_heads = pairs.shape[1] // (2 * HEAD_SIZE)
    steps = width // (heads_per_step * HEAD_SIZE)
    per_kv = steps // kv_heads
    block = (rows, heads_per_step * HEAD_SIZE)
    return pl.pallas_call(
        attention_kernel,
        grid=(steps,),
        in_specs=[
            pl.BlockSpec(memory_space=pltpu.SMEM),
            pl.BlockSpec(block, lambda i: (0, i)),
            pl.BlockSpec((length, HEAD_SIZE), lambda i: (0, i // per_kv)),
            pl.BlockSpec((length, HEAD_SIZE), lambda i: (0, kv_heads + i // per_kv)),
        ],
        out_specs=pl.BlockSpec(block, lambda i: (0, i)),
        out_shape=jax.ShapeDtypeStruct(queries.shape, BF),
        compiler_params=pltpu.CompilerParams(vmem_limit_bytes=VMEM),
        cost_estimate=pl.CostEstimate(
            flops=4 * rows * width * length, bytes_accessed=9_000_000, transcendentals=rows * length * width // HEAD_SIZE
        ),
        name="attention_rows",
    )(first, queries, pairs, pairs)


def on_device(queries, keys, values, tokens, routed, gates, up, down):
    pairs = jnp.concatenate([keys[0], values[0]], axis=1)
    pairs = lax.all_gather(pairs, "seq", axis=0, tiled=True)
    everywhere = ("seq", "exp")
    outgoing = dispatch(routed.T, tokens)
    arrived = lax.all_to_all(outgoing, everywhere, split_axis=0, concat_axis=0, tiled=True)
    arrived, pairs = lax.optimization_barrier((arrived, pairs))
    made = run_experts(arrived, up, down)
    made, own, routed, gates = lax.optimization_barrier((made, queries[0], routed, gates))
    returned = lax.all_to_all(made, everywhere, split_axis=0, concat_axis=0, tiled=True)
    weights = gate_matrix(routed.T, gates.T)
    first = (lax.axis_index("seq") * own.shape[0]).astype(jnp.int32).reshape(1)
    attended = attention(first, own, pairs)
    return (attended[None], combine(weights, returned))


def solution(mesh):
    spread = P(("seq", "exp"), None)
    in_specs = (P("exp", "seq", None),) * 3 + (spread,) * 3 + (P(("seq", "exp"), None, None),) * 2
    out_specs = (P("exp", "seq", None), spread)
    return jax.shard_map(on_device, mesh=mesh, in_specs=in_specs, out_specs=out_specs, check_vma=False)
```

```python
import functools

import jax
import jax.numpy as jnp
from jax import lax
from jax.experimental import pallas as pl
from jax.experimental.pallas import tpu as pltpu
from jax.sharding import PartitionSpec as P

HEAD_SIZE = 128
HALF = 4
LAST = 8
FOLD = 512
BF = jnp.bfloat16
F32 = jnp.float32
VMEM = 56 * 1024 * 1024


def iota(shape, dim):
    return lax.broadcasted_iota(jnp.int32, shape, dim)


def dot(a, b):
    return jnp.dot(a, b, preferred_element_type=F32)


def permutation(source):
    row, col = iota((256, 256), 0), iota((256, 256), 1)
    return (col == source(row)).astype(F32).astype(BF)


def fold_matrix():
    return permutation(lambda i: (i & 7) * 32 + (i >> 3))


def unfold_matrix():
    return permutation(lambda i: (i & 31) * 8 + (i >> 5))


def fold_half_matrix():
    return permutation(lambda i: ((i >> 2) & 1) * 128 + (i >> 3) * 4 + (i & 3))


def unfold_half_matrix():
    return permutation(lambda i: ((i >> 2) & 31) * 8 + (i >> 7) * 4 + (i & 3))


def ranks(routed):
    tokens = routed.shape[1]
    experts = iota((128, tokens), 0)
    named = jnp.zeros((128, tokens), F32)
    for j in range(routed.shape[0]):
        named = jnp.where(routed[j : j + 1, :] == experts, 1.0, named)
    earlier = (iota((tokens, tokens), 0) < iota((tokens, tokens), 1)).astype(F32).astype(BF)
    before = dot(named.astype(BF), earlier)
    return jnp.where(named > 0.5, before, -1.0)


def block_copy(source, target, b, columns, sem):
    rows = pl.ds(b * 256, 256)
    return pltpu.make_async_copy(source.at[rows, :], target.at[rows, columns], sem)


def dispatch_kernel(
    routed_ref, tokens_hbm, out_hbm, tokens_ref, rows_ref, ninth_ref, fold_ref, in_sems, sems, *, first, ninth
):
    half = tokens_ref.shape[1]
    parts = half // FOLD
    loads = [
        pltpu.make_async_copy(
            tokens_hbm.at[:, pl.ds(h * half, half)], tokens_ref.at[pl.ds(h * 128, 128), :], in_sems.at[h]
        )
        for h in range(2)
    ]
    for load in loads:
        load.start()
    rank = ranks(routed_ref[...])
    low = rank.astype(BF)
    row = iota((256, 128), 0)
    slot = ((row & 3) + first).astype(F32)
    upper = ((row >> 2) & 1) == 1
    copies = []
    for b in range(4):
        expand = (iota((256, 128), 1) == b * 32 + (row >> 3)).astype(F32).astype(BF)
        band = jnp.where(dot(expand, low) == slot, 1.0, 0.0)
        pick = jnp.concatenate([jnp.where(upper, 0.0, band), jnp.where(upper, band, 0.0)], axis=1).astype(BF)
        if b == 0:
            for load in loads:
                load.wait()
        for c in range(parts):
            cols = slice(c * FOLD, (c + 1) * FOLD)
            rows_ref[b * 256 : (b + 1) * 256, cols] = dot(pick, tokens_ref[:, cols]).astype(BF)
        copies.append(block_copy(rows_ref, out_hbm, b, pl.ds(0, half), sems.at[b, 0]))
        copies[-1].start()
    if ninth:
        pick = jnp.where(rank == float(LAST), 1.0, 0.0).astype(BF)
        for r in range(2 * parts):
            h, c = divmod(r, parts)
            ninth_ref[r] = dot(pick, tokens_ref[h * 128 : (h + 1) * 128, c * FOLD : (c + 1) * FOLD]).astype(BF)
        fold = fold_matrix()
        for b in range(4):
            piece = jnp.concatenate([ninth_ref[r, b * 32 : (b + 1) * 32, :] for r in range(8)], axis=0)
            fold_ref[b * 256 : (b + 1) * 256, :] = dot(fold, piece).astype(BF)
            copies.append(block_copy(fold_ref, out_hbm, b, pl.ds(half, FOLD), sems.at[b, 1]))
            copies[-1].start()
    for copy in copies:
        copy.wait()


def dispatch(routed, tokens, second):
    half = tokens.shape[1] // 2
    return pl.pallas_call(
        functools.partial(dispatch_kernel, first=HALF * second, ninth=second),
        in_specs=[pl.BlockSpec(memory_space=pltpu.VMEM), pl.BlockSpec(memory_space=pl.ANY)],
        out_specs=pl.BlockSpec(memory_space=pl.ANY),
        out_shape=jax.ShapeDtypeStruct((1024, half + FOLD * second), BF),
        scratch_shapes=[
            pltpu.VMEM((256, half), BF),
            pltpu.VMEM((1024, half), BF),
            pltpu.VMEM((8, 128, FOLD), BF),
            pltpu.VMEM((1024, FOLD), BF),
            pltpu.SemaphoreType.DMA((2,)),
            pltpu.SemaphoreType.DMA((4, 2)),
        ],
        compiler_params=pltpu.CompilerParams(vmem_limit_bytes=VMEM),
        cost_estimate=pl.CostEstimate(flops=2 * 640 * 128 * 4096, bytes_accessed=6_000_000, transcendentals=0),
        name="dispatch_rows",
    )(routed, tokens)


def gates_kernel(routed_ref, gates_ref, first_ref, second_ref, ninth_ref):
    routed = routed_ref[...]
    tokens = routed.shape[1]
    rank = ranks(routed)
    experts = iota((128, tokens), 0)
    gate = jnp.zeros((128, tokens), F32)
    for j in range(routed.shape[0]):
        gate = jnp.where(routed[j : j + 1, :] == experts, gates_ref[j : j + 1, :], gate)
    gate = gate.T
    rank = rank.T
    high = gate.astype(BF)
    low = (gate - high.astype(F32)).astype(BF)
    expand = (iota((128, 1024), 0) == (iota((128, 1024), 1) >> 3)).astype(F32).astype(BF)
    spread = dot(rank.astype(BF), expand)
    lane = iota((tokens, 1024), 1)
    slot = (lane & 3).astype(F32)
    for part, value in enumerate((high, low)):
        wide = dot(value, expand)
        ninth_ref[part * tokens : (part + 1) * tokens, :] = jnp.where(
            rank == float(LAST), value.astype(F32), 0.0
        ).astype(BF)
        for h in range(2):
            rows = slice((part * 2 + h) * tokens, (part * 2 + h + 1) * tokens)
            kept = jnp.where(((lane >> 2) & 1) == h, wide, 0.0)
            first_ref[rows, :] = jnp.where(spread == slot, kept, 0.0).astype(BF)
            second_ref[rows, :] = jnp.where(spread == slot + float(HALF), kept, 0.0).astype(BF)


def gate_matrices(routed, gates):
    tokens = routed.shape[1]
    shape = jax.ShapeDtypeStruct((4 * tokens, 1024), BF)
    return pl.pallas_call(
        gates_kernel,
        out_shape=(shape, shape, jax.ShapeDtypeStruct((2 * tokens, 128), BF)),
        compiler_params=pltpu.CompilerParams(vmem_limit_bytes=VMEM),
        cost_estimate=pl.CostEstimate(flops=6 * 128 * 128 * 1024, bytes_accessed=2_200_000, transcendentals=0),
        name="gate_matrices",
    )(routed, gates)


def experts_kernel(
    rows_hbm, up_hbm, down_hbm, out_hbm,
    stage_ref, last_ref, rows_ref, up_ref, down_ref, hidden_ref, made_ref, sent_ref, fold_ref,
    row_sems, up_sems, down_sems, sems,
    *, ninth, part,
):
    half = stage_ref.shape[1]
    width = rows_ref.shape[1]
    units = hidden_ref.shape[1]
    count = rows_ref.shape[0] // 4
    parts = half // FOLD
    chunks = up_sems.shape[0]
    deep = width // chunks

    row_loads = []
    for b in range(4):
        rows = pl.ds(b * 256, 256)
        loads = [pltpu.make_async_copy(rows_hbm.at[rows, pl.ds(0, half)], stage_ref.at[rows, :], row_sems.at[b, 0])]
        if ninth:
            loads.append(
                pltpu.make_async_copy(rows_hbm.at[rows, pl.ds(half, FOLD)], last_ref.at[rows, :], row_sems.at[b, 1])
            )
        row_loads.append(loads)
    up_loads = [
        pltpu.make_async_copy(
            up_hbm.at[0, pl.ds(k * deep, deep), :], up_ref.at[pl.ds(k * deep, deep), :], up_sems.at[k]
        )
        for k in range(chunks)
    ]
    down_load = pltpu.make_async_copy(down_hbm.at[0], down_ref, down_sems.at[0])
    for loads in row_loads:
        for load in loads:
            load.start()
    for load in up_loads:
        load.start()
    down_load.start()

    unfold_half = unfold_half_matrix()
    for b in range(4):
        for load in row_loads[b]:
            load.wait()
        for c in range(parts):
            cols = slice(c * FOLD, (c + 1) * FOLD)
            both = dot(unfold_half, stage_ref[b * 256 : (b + 1) * 256, cols]).astype(BF)
            rows_ref[b * count : b * count + 128, cols] = both[:128]
            rows_ref[b * count : b * count + 128, half + c * FOLD : half + (c + 1) * FOLD] = both[128:]
        if ninth:
            piece = dot(unfold_matrix(), last_ref[b * 256 : (b + 1) * 256, :]).astype(BF)
            for r in range(8):
                rows_ref[b * count + 128 : (b + 1) * count, r * FOLD : (r + 1) * FOLD] = piece[r * 32 : (r + 1) * 32]
    for load in up_loads:
        load.wait()
    for c in range(units // part):
        cols = slice(c * part, (c + 1) * part)
        gate = dot(rows_ref[...], up_ref[:, cols])
        linear = dot(rows_ref[...], up_ref[:, units + c * part : units + (c + 1) * part])
        hidden_ref[:, cols] = (gate / (1.0 + jnp.exp(-gate)) * linear).astype(BF)
    down_load.wait()
    for c in range(width // FOLD):
        cols = slice(c * FOLD, (c + 1) * FOLD)
        made_ref[:, cols] = dot(hidden_ref[...], down_ref[:, cols]).astype(BF)
    copies = []
    fold_half = fold_half_matrix()
    for b in range(4):
        rows = slice(b * count, b * count + 128)
        for c in range(parts):
            cols = slice(c * FOLD, (c + 1) * FOLD)
            piece = jnp.concatenate(
                [made_ref[rows, cols], made_ref[rows, half + c * FOLD : half + (c + 1) * FOLD]], axis=0
            )
            sent_ref[b * 256 : (b + 1) * 256, cols] = dot(fold_half, piece).astype(BF)
        copies.append(block_copy(sent_ref, out_hbm, b, pl.ds(0, half), sems.at[b, 0]))
        copies[-1].start()
        if ninth:
            rows = slice(b * count + 128, (b + 1) * count)
            piece = jnp.concatenate([made_ref[rows, r * FOLD : (r + 1) * FOLD] for r in range(8)], axis=0)
            fold_ref[b * 256 : (b + 1) * 256, :] = dot(fold_matrix(), piece).astype(BF)
            copies.append(block_copy(fold_ref, out_hbm, b, pl.ds(half, FOLD), sems.at[b, 1]))
            copies[-1].start()
    for copy in copies:
        copy.wait()


def run_experts(arrived, up, down, part=256, chunks=4):
    width = up.shape[1]
    units = down.shape[1]
    half = width // 2
    ninth = arrived.shape[1] > half
    all_rows = 4 * (160 if ninth else 128)
    return pl.pallas_call(
        functools.partial(experts_kernel, ninth=ninth, part=part),
        in_specs=[pl.BlockSpec(memory_space=pl.ANY)] * 3,
        out_specs=pl.BlockSpec(memory_space=pl.ANY),
        out_shape=jax.ShapeDtypeStruct(arrived.shape, BF),
        scratch_shapes=[
            pltpu.VMEM((1024, half), BF),
            pltpu.VMEM((1024, FOLD), BF),
            pltpu.VMEM((all_rows, width), BF),
            pltpu.VMEM((width, 2 * units), BF),
            pltpu.VMEM((units, width), BF),
            pltpu.VMEM((all_rows, units), BF),
            pltpu.VMEM((all_rows, width), BF),
            pltpu.VMEM((1024, half), BF),
            pltpu.VMEM((1024, FOLD), BF),
            pltpu.SemaphoreType.DMA((4, 2)),
            pltpu.SemaphoreType.DMA((chunks,)),
            pltpu.SemaphoreType.DMA((1,)),
            pltpu.SemaphoreType.DMA((4, 2)),
        ],
        compiler_params=pltpu.CompilerParams(vmem_limit_bytes=VMEM),
        cost_estimate=pl.CostEstimate(
            flops=2 * all_rows * units * 3 * width, bytes_accessed=29_000_000, transcendentals=all_rows * units
        ),
        name="run_experts",
    )(arrived, up, down)


def first_combine_kernel(gates_ref, rows_ref, out_ref):
    tokens, width = out_ref.shape
    half = width // 2
    for c in range(half // FOLD):
        both = dot(gates_ref[...], rows_ref[:, c * FOLD : (c + 1) * FOLD])
        for h in range(2):
            at = h * half + c * FOLD
            out_ref[:, at : at + FOLD] = (
                both[h * tokens : (h + 1) * tokens] + both[(2 + h) * tokens : (3 + h) * tokens]
            )


def first_combine(gates, returned):
    tokens = gates.shape[0] // 4
    return pl.pallas_call(
        first_combine_kernel,
        out_shape=jax.ShapeDtypeStruct((tokens, 2 * returned.shape[1]), F32),
        compiler_params=pltpu.CompilerParams(vmem_limit_bytes=VMEM),
        cost_estimate=pl.CostEstimate(flops=2 * 512 * 1024 * 2048, bytes_accessed=7_500_000, transcendentals=0),
        name="first_combine",
    )(gates, returned)


def last_combine_kernel(
    gates_hbm, ninth_hbm, sum_hbm, rows_hbm, out_hbm,
    gates_ref, ninth_ref, sum_ref, rows_ref, last_ref, out_ref, row_sems, sems, out_sems,
):
    tokens, width = out_ref.shape
    half = width // 2
    parts = half // FOLD
    row_loads = []
    for b in range(4):
        rows = pl.ds(b * 256, 256)
        row_loads.append(pltpu.make_async_copy(rows_hbm.at[rows, :], rows_ref.at[rows, :], row_sems.at[b]))
        row_loads[-1].start()
    loads = [
        pltpu.make_async_copy(ninth_hbm, ninth_ref, sems.at[0]),
        pltpu.make_async_copy(gates_hbm, gates_ref, sems.at[1]),
        pltpu.make_async_copy(sum_hbm, sum_ref, sems.at[2]),
    ]
    for load in loads:
        load.start()
    unfold = unfold_matrix()
    for b in range(4):
        row_loads[b].wait()
        piece = dot(unfold, rows_ref[b * 256 : (b + 1) * 256, half:]).astype(BF)
        for r in range(8):
            last_ref[r, b * 32 : (b + 1) * 32, :] = piece[r * 32 : (r + 1) * 32]
    for load in loads:
        load.wait()
    copies = []
    for c in range(parts):
        both = dot(gates_ref[...], rows_ref[:, c * FOLD : (c + 1) * FOLD])
        for h in range(2):
            at = h * half + c * FOLD
            more = dot(ninth_ref[...], last_ref[h * parts + c])
            out_ref[:, at : at + FOLD] = (
                sum_ref[:, at : at + FOLD]
                + both[h * tokens : (h + 1) * tokens] + both[(2 + h) * tokens : (3 + h) * tokens]
                + more[:tokens] + more[tokens:]
            ).astype(BF)
            cols = pl.ds(at, FOLD)
            copies.append(pltpu.make_async_copy(out_ref.at[:, cols], out_hbm.at[:, cols], out_sems.at[c, h]))
            copies[-1].start()
    for copy in copies:
        copy.wait()


def last_combine(gates, ninth, total, returned):
    rows = returned.shape[0]
    tokens, width = total.shape
    return pl.pallas_call(
        last_combine_kernel,
        in_specs=[pl.BlockSpec(memory_space=pl.ANY)] * 4,
        out_specs=pl.BlockSpec(memory_space=pl.ANY),
        out_shape=jax.ShapeDtypeStruct((tokens, width), BF),
        scratch_shapes=[
            pltpu.VMEM(gates.shape, BF),
            pltpu.VMEM(ninth.shape, BF),
            pltpu.VMEM(total.shape, F32),
            pltpu.VMEM(returned.shape, BF),
            pltpu.VMEM((8, 128, FOLD), BF),
            pltpu.VMEM((tokens, width), BF),
            pltpu.SemaphoreType.DMA((rows // 256,)),
            pltpu.SemaphoreType.DMA((3,)),
            pltpu.SemaphoreType.DMA((width // 2 // FOLD, 2)),
        ],
        compiler_params=pltpu.CompilerParams(vmem_limit_bytes=VMEM),
        cost_estimate=pl.CostEstimate(flops=2 * 512 * 1152 * 2048, bytes_accessed=10_000_000, transcendentals=0),
        name="last_combine",
    )(gates, ninth, total, returned)


def attention_kernel(place_ref, queries_ref, keys_ref, values_ref, out_ref):
    rows = queries_ref.shape[0]
    heads = queries_ref.shape[1] // HEAD_SIZE
    ahead = iota((rows, rows), 1) - iota((rows, rows), 0)
    seen = jnp.concatenate(
        [ahead <= (place_ref[0] - place_ref[j]) * rows for j in range(keys_ref.shape[0] // rows)], axis=1
    )
    factor = HEAD_SIZE**-0.5 * 1.4426950408889634
    for h in range(heads):
        cols = slice(h * HEAD_SIZE, (h + 1) * HEAD_SIZE)
        scores = lax.dot_general(
            queries_ref[:, cols], keys_ref[...], (((1,), (1,)), ((), ())), preferred_element_type=F32
        )
        scores = jnp.where(seen, scores, -1e30)
        top = jnp.max(scores, axis=-1, keepdims=True)
        part = jnp.exp2((scores - top) * factor)
        total = jnp.sum(part, axis=-1, keepdims=True)
        mixed = dot(part.astype(BF), values_ref[...])
        out_ref[:, cols] = (mixed / total).astype(BF)


def attention(places, queries, pairs, heads_per_step=16):
    rows, width = queries.shape
    length = pairs.shape[0]
    kv_heads = pairs.shape[1] // (2 * HEAD_SIZE)
    steps = width // (heads_per_step * HEAD_SIZE)
    per_kv = steps // kv_heads
    block = (rows, heads_per_step * HEAD_SIZE)
    return pl.pallas_call(
        attention_kernel,
        grid=(steps,),
        in_specs=[
            pl.BlockSpec(memory_space=pltpu.SMEM),
            pl.BlockSpec(block, lambda i: (0, i)),
            pl.BlockSpec((length, HEAD_SIZE), lambda i: (0, i // per_kv)),
            pl.BlockSpec((length, HEAD_SIZE), lambda i: (0, kv_heads + i // per_kv)),
        ],
        out_specs=pl.BlockSpec(block, lambda i: (0, i)),
        out_shape=jax.ShapeDtypeStruct(queries.shape, BF),
        compiler_params=pltpu.CompilerParams(vmem_limit_bytes=VMEM),
        cost_estimate=pl.CostEstimate(
            flops=4 * rows * width * length, bytes_accessed=9_000_000, transcendentals=rows * length * width // HEAD_SIZE
        ),
        name="attention_rows",
    )(places, queries, pairs, pairs)


def at(y, z, core):
    return y * 8 + (z % 4) * 2 + core


def moved(rows, dy=0, dz=0, dcore=0):
    pairs = [
        (at(y, z, core), at((y + dy) % 2, z + dz, (core + dcore) % 2))
        for y in range(2) for z in range(4) for core in range(2)
    ]
    return lax.ppermute(rows, "seq", pairs)


def exchange(rows):
    return lax.all_to_all(rows, ("seq", "exp"), split_axis=0, concat_axis=0, tiled=True)


def on_device(queries, keys, values, tokens, routed, gates, up, down):
    tied = lax.optimization_barrier
    block = keys.shape[1]
    routed, gates = routed.T, gates.T
    pairs = jnp.concatenate([keys[0], values[0]], axis=1)
    across = moved(pairs, dy=1)
    outgoing = dispatch(routed, tokens, False)

    outgoing, pairs, across, routed, tokens = tied((outgoing, pairs, across, routed, tokens))
    arrived_1 = exchange(outgoing)
    outgoing = dispatch(routed, tokens, True)
    here = jnp.concatenate([pairs, across], axis=0)
    below, above = moved(here, dz=1), moved(here, dz=-1)

    arrived_1, outgoing, here, below, above = tied((arrived_1, outgoing, here, below, above))
    arrived_2 = exchange(outgoing)
    made = run_experts(arrived_1, up, down)
    far = [moved(below[:block], dz=1), moved(above[block:], dz=-1)]

    arrived_2, made, here, below, above, far = tied((arrived_2, made, here, below, above, far))
    returned_1 = exchange(made)
    made = run_experts(arrived_2, up, down)
    column = jnp.concatenate([here, below, above, *far], axis=0)
    other = moved(column, dcore=1)

    returned_1, made, column, other, routed, gates, own = tied(
        (returned_1, made, column, other, routed, gates, queries[0])
    )
    returned_2 = exchange(made)
    weights_1, weights_2, weights_3 = gate_matrices(routed, gates)
    total = first_combine(weights_1, returned_1)
    index = lax.axis_index("seq")
    y, z, core = index // 8, index // 2 % 4, index % 2
    places = [
        at((y + dy) % 2, z + dz, (core + dcore) % 2) for dcore in range(2) for dz in (0, -1, 1, 2) for dy in range(2)
    ]
    whole = jnp.concatenate([column, other], axis=0)
    attended = attention(jnp.stack(places).astype(jnp.int32), own, whole)
    return (attended[None], last_combine(weights_2, weights_3, total, returned_2))


def solution(mesh):
    spread = P(("seq", "exp"), None)
    in_specs = (P("exp", "seq", None),) * 3 + (spread,) * 3 + (P(("seq", "exp"), None, None),) * 2
    out_specs = (P("exp", "seq", None), spread)
    return jax.shard_map(on_device, mesh=mesh, in_specs=in_specs, out_specs=out_specs, check_vma=False)
```

```python
import functools

import jax
import jax.numpy as jnp
from jax import lax
from jax.experimental import pallas as pl
from jax.experimental.pallas import tpu as pltpu
from jax.sharding import PartitionSpec as P

HEAD_SIZE = 128
HALF = 4
LAST = 8
FOLD = 512
BF = jnp.bfloat16
F32 = jnp.float32
VMEM = 56 * 1024 * 1024


def iota(shape, dim):
    return lax.broadcasted_iota(jnp.int32, shape, dim)


def dot(a, b):
    return jnp.dot(a, b, preferred_element_type=F32)


def permutation(source):
    row, col = iota((256, 256), 0), iota((256, 256), 1)
    return (col == source(row)).astype(F32).astype(BF)


def fold_matrix():
    return permutation(lambda i: (i & 7) * 32 + (i >> 3))


def unfold_matrix():
    return permutation(lambda i: (i & 31) * 8 + (i >> 5))


def fold_half_matrix():
    return permutation(lambda i: ((i >> 2) & 1) * 128 + (i >> 3) * 4 + (i & 3))


def unfold_half_matrix():
    return permutation(lambda i: ((i >> 2) & 31) * 8 + (i >> 7) * 4 + (i & 3))


def ranks(routed):
    tokens = routed.shape[1]
    experts = iota((128, tokens), 0)
    named = jnp.zeros((128, tokens), F32)
    for j in range(routed.shape[0]):
        named = jnp.where(routed[j : j + 1, :] == experts, 1.0, named)
    earlier = (iota((tokens, tokens), 0) < iota((tokens, tokens), 1)).astype(F32).astype(BF)
    before = dot(named.astype(BF), earlier)
    return jnp.where(named > 0.5, before, -1.0)


def block_copy(source, target, b, columns, sem):
    rows = pl.ds(b * 256, 256)
    return pltpu.make_async_copy(source.at[rows, :], target.at[rows, columns], sem)


def dispatch_kernel(
    routed_hbm, tokens_hbm, out_hbm, routed_ref, tokens_ref, rows_ref, ninth_ref, fold_ref, in_sems, sems, *, first, ninth
):
    half = tokens_ref.shape[1]
    parts = half // FOLD
    loads = [
        pltpu.make_async_copy(
            tokens_hbm.at[:, pl.ds(h * half, half)], tokens_ref.at[pl.ds(h * 128, 128), :], in_sems.at[h]
        )
        for h in range(2)
    ]
    named = pltpu.make_async_copy(routed_hbm, routed_ref, in_sems.at[2])
    for load in (named, *loads):
        load.start()
    named.wait()
    rank = ranks(routed_ref[...])
    low = rank.astype(BF)
    row = iota((256, 128), 0)
    slot = ((row & 3) + first).astype(F32)
    upper = ((row >> 2) & 1) == 1
    copies = []
    for b in range(4):
        expand = (iota((256, 128), 1) == b * 32 + (row >> 3)).astype(F32).astype(BF)
        band = jnp.where(dot(expand, low) == slot, 1.0, 0.0)
        pick = jnp.concatenate([jnp.where(upper, 0.0, band), jnp.where(upper, band, 0.0)], axis=1).astype(BF)
        if b == 0:
            for load in loads:
                load.wait()
        for c in range(parts):
            cols = slice(c * FOLD, (c + 1) * FOLD)
            rows_ref[b * 256 : (b + 1) * 256, cols] = dot(pick, tokens_ref[:, cols]).astype(BF)
        copies.append(block_copy(rows_ref, out_hbm, b, pl.ds(0, half), sems.at[b, 0]))
        copies[-1].start()
    if ninth:
        pick = jnp.where(rank == float(LAST), 1.0, 0.0).astype(BF)
        for r in range(2 * parts):
            h, c = divmod(r, parts)
            ninth_ref[r] = dot(pick, tokens_ref[h * 128 : (h + 1) * 128, c * FOLD : (c + 1) * FOLD]).astype(BF)
        fold = fold_matrix()
        for b in range(4):
            piece = jnp.concatenate([ninth_ref[r, b * 32 : (b + 1) * 32, :] for r in range(8)], axis=0)
            fold_ref[b * 256 : (b + 1) * 256, :] = dot(fold, piece).astype(BF)
            copies.append(block_copy(fold_ref, out_hbm, b, pl.ds(half, FOLD), sems.at[b, 1]))
            copies[-1].start()
    for copy in copies:
        copy.wait()


def dispatch(routed, tokens, second):
    half = tokens.shape[1] // 2
    return pl.pallas_call(
        functools.partial(dispatch_kernel, first=HALF * second, ninth=second),
        in_specs=[pl.BlockSpec(memory_space=pl.ANY)] * 2,
        out_specs=pl.BlockSpec(memory_space=pl.ANY),
        out_shape=jax.ShapeDtypeStruct((1024, half + FOLD * second), BF),
        scratch_shapes=[
            pltpu.VMEM(routed.shape, jnp.int32),
            pltpu.VMEM((256, half), BF),
            pltpu.VMEM((1024, half), BF),
            pltpu.VMEM((8, 128, FOLD), BF),
            pltpu.VMEM((1024, FOLD), BF),
            pltpu.SemaphoreType.DMA((3,)),
            pltpu.SemaphoreType.DMA((4, 2)),
        ],
        compiler_params=pltpu.CompilerParams(vmem_limit_bytes=VMEM),
        cost_estimate=pl.CostEstimate(flops=2 * 640 * 128 * 4096, bytes_accessed=6_000_000, transcendentals=0),
        name="dispatch_rows",
    )(routed, tokens)


def gates_kernel(routed_ref, gates_ref, first_ref, second_ref, ninth_ref):
    routed = routed_ref[...]
    tokens = routed.shape[1]
    rank = ranks(routed)
    experts = iota((128, tokens), 0)
    gate = jnp.zeros((128, tokens), F32)
    for j in range(routed.shape[0]):
        gate = jnp.where(routed[j : j + 1, :] == experts, gates_ref[j : j + 1, :], gate)
    gate = gate.T
    rank = rank.T
    high = gate.astype(BF)
    low = (gate - high.astype(F32)).astype(BF)
    expand = (iota((128, 1024), 0) == (iota((128, 1024), 1) >> 3)).astype(F32).astype(BF)
    spread = dot(rank.astype(BF), expand)
    lane = iota((tokens, 1024), 1)
    slot = (lane & 3).astype(F32)
    for part, value in enumerate((high, low)):
        wide = dot(value, expand)
        ninth_ref[part * tokens : (part + 1) * tokens, :] = jnp.where(
            rank == float(LAST), value.astype(F32), 0.0
        ).astype(BF)
        for h in range(2):
            rows = slice((part * 2 + h) * tokens, (part * 2 + h + 1) * tokens)
            kept = jnp.where(((lane >> 2) & 1) == h, wide, 0.0)
            first_ref[rows, :] = jnp.where(spread == slot, kept, 0.0).astype(BF)
            second_ref[rows, :] = jnp.where(spread == slot + float(HALF), kept, 0.0).astype(BF)


def gate_matrices(routed, gates):
    tokens = routed.shape[1]
    shape = jax.ShapeDtypeStruct((4 * tokens, 1024), BF)
    return pl.pallas_call(
        gates_kernel,
        out_shape=(shape, shape, jax.ShapeDtypeStruct((2 * tokens, 128), BF)),
        compiler_params=pltpu.CompilerParams(vmem_limit_bytes=VMEM),
        cost_estimate=pl.CostEstimate(flops=6 * 128 * 128 * 1024, bytes_accessed=2_200_000, transcendentals=0),
        name="gate_matrices",
    )(routed, gates)


def experts_kernel(
    rows_hbm, up_hbm, down_hbm, out_hbm,
    stage_ref, last_ref, rows_ref, up_ref, down_ref, hidden_ref, made_ref, sent_ref, fold_ref,
    row_sems, up_sems, down_sems, sems,
    *, ninth, part,
):
    half = stage_ref.shape[1]
    width = rows_ref.shape[1]
    units = hidden_ref.shape[1]
    count = rows_ref.shape[0] // 4
    parts = half // FOLD
    chunks = up_sems.shape[0]
    deep = width // chunks

    row_loads = []
    for b in range(4):
        rows = pl.ds(b * 256, 256)
        loads = [pltpu.make_async_copy(rows_hbm.at[rows, pl.ds(0, half)], stage_ref.at[rows, :], row_sems.at[b, 0])]
        if ninth:
            loads.append(
                pltpu.make_async_copy(rows_hbm.at[rows, pl.ds(half, FOLD)], last_ref.at[rows, :], row_sems.at[b, 1])
            )
        row_loads.append(loads)
    up_loads = [
        pltpu.make_async_copy(
            up_hbm.at[0, pl.ds(k * deep, deep), :], up_ref.at[pl.ds(k * deep, deep), :], up_sems.at[k]
        )
        for k in range(chunks)
    ]
    down_load = pltpu.make_async_copy(down_hbm.at[0], down_ref, down_sems.at[0])
    for loads in row_loads:
        for load in loads:
            load.start()
    for load in up_loads:
        load.start()
    down_load.start()

    unfold_half = unfold_half_matrix()
    for b in range(4):
        for load in row_loads[b]:
            load.wait()
        for c in range(parts):
            cols = slice(c * FOLD, (c + 1) * FOLD)
            both = dot(unfold_half, stage_ref[b * 256 : (b + 1) * 256, cols]).astype(BF)
            rows_ref[b * count : b * count + 128, cols] = both[:128]
            rows_ref[b * count : b * count + 128, half + c * FOLD : half + (c + 1) * FOLD] = both[128:]
        if ninth:
            piece = dot(unfold_matrix(), last_ref[b * 256 : (b + 1) * 256, :]).astype(BF)
            for r in range(8):
                rows_ref[b * count + 128 : (b + 1) * count, r * FOLD : (r + 1) * FOLD] = piece[r * 32 : (r + 1) * 32]
    for load in up_loads:
        load.wait()
    for c in range(units // part):
        cols = slice(c * part, (c + 1) * part)
        gate = dot(rows_ref[...], up_ref[:, cols])
        linear = dot(rows_ref[...], up_ref[:, units + c * part : units + (c + 1) * part])
        hidden_ref[:, cols] = (gate / (1.0 + jnp.exp(-gate)) * linear).astype(BF)
    down_load.wait()
    for c in range(width // FOLD):
        cols = slice(c * FOLD, (c + 1) * FOLD)
        made_ref[:, cols] = dot(hidden_ref[...], down_ref[:, cols]).astype(BF)
    copies = []
    fold_half = fold_half_matrix()
    for b in range(4):
        rows = slice(b * count, b * count + 128)
        for c in range(parts):
            cols = slice(c * FOLD, (c + 1) * FOLD)
            piece = jnp.concatenate(
                [made_ref[rows, cols], made_ref[rows, half + c * FOLD : half + (c + 1) * FOLD]], axis=0
            )
            sent_ref[b * 256 : (b + 1) * 256, cols] = dot(fold_half, piece).astype(BF)
        copies.append(block_copy(sent_ref, out_hbm, b, pl.ds(0, half), sems.at[b, 0]))
        copies[-1].start()
        if ninth:
            rows = slice(b * count + 128, (b + 1) * count)
            piece = jnp.concatenate([made_ref[rows, r * FOLD : (r + 1) * FOLD] for r in range(8)], axis=0)
            fold_ref[b * 256 : (b + 1) * 256, :] = dot(fold_matrix(), piece).astype(BF)
            copies.append(block_copy(fold_ref, out_hbm, b, pl.ds(half, FOLD), sems.at[b, 1]))
            copies[-1].start()
    for copy in copies:
        copy.wait()


def run_experts(arrived, up, down, part=256, chunks=4):
    width = up.shape[1]
    units = down.shape[1]
    half = width // 2
    ninth = arrived.shape[1] > half
    all_rows = 4 * (160 if ninth else 128)
    return pl.pallas_call(
        functools.partial(experts_kernel, ninth=ninth, part=part),
        in_specs=[pl.BlockSpec(memory_space=pl.ANY)] * 3,
        out_specs=pl.BlockSpec(memory_space=pl.ANY),
        out_shape=jax.ShapeDtypeStruct(arrived.shape, BF),
        scratch_shapes=[
            pltpu.VMEM((1024, half), BF),
            pltpu.VMEM((1024, FOLD), BF),
            pltpu.VMEM((all_rows, width), BF),
            pltpu.VMEM((width, 2 * units), BF),
            pltpu.VMEM((units, width), BF),
            pltpu.VMEM((all_rows, units), BF),
            pltpu.VMEM((all_rows, width), BF),
            pltpu.VMEM((1024, half), BF),
            pltpu.VMEM((1024, FOLD), BF),
            pltpu.SemaphoreType.DMA((4, 2)),
            pltpu.SemaphoreType.DMA((chunks,)),
            pltpu.SemaphoreType.DMA((1,)),
            pltpu.SemaphoreType.DMA((4, 2)),
        ],
        compiler_params=pltpu.CompilerParams(vmem_limit_bytes=VMEM),
        cost_estimate=pl.CostEstimate(
            flops=2 * all_rows * units * 3 * width, bytes_accessed=29_000_000, transcendentals=all_rows * units
        ),
        name="run_experts",
    )(arrived, up, down)


def first_combine_kernel(gates_ref, rows_ref, out_ref):
    tokens, width = out_ref.shape
    half = width // 2
    for c in range(half // FOLD):
        both = dot(gates_ref[...], rows_ref[:, c * FOLD : (c + 1) * FOLD])
        for h in range(2):
            at = h * half + c * FOLD
            out_ref[:, at : at + FOLD] = (
                both[h * tokens : (h + 1) * tokens] + both[(2 + h) * tokens : (3 + h) * tokens]
            )


def first_combine(gates, returned):
    tokens = gates.shape[0] // 4
    return pl.pallas_call(
        first_combine_kernel,
        out_shape=jax.ShapeDtypeStruct((tokens, 2 * returned.shape[1]), F32),
        compiler_params=pltpu.CompilerParams(vmem_limit_bytes=VMEM),
        cost_estimate=pl.CostEstimate(flops=2 * 512 * 1024 * 2048, bytes_accessed=7_500_000, transcendentals=0),
        name="first_combine",
    )(gates, returned)


def last_combine_kernel(
    gates_hbm, ninth_hbm, sum_hbm, rows_hbm, out_hbm,
    gates_ref, ninth_ref, sum_ref, rows_ref, last_ref, part_ref, out_ref, row_sems, sems, out_sems,
):
    tokens, width = out_ref.shape
    half = width // 2
    parts = half // FOLD
    loads = [
        pltpu.make_async_copy(gates_hbm, gates_ref, sems.at[0]),
        pltpu.make_async_copy(ninth_hbm, ninth_ref, sems.at[1]),
        pltpu.make_async_copy(sum_hbm, sum_ref, sems.at[2]),
    ]
    row_loads = []
    for b in range(4):
        rows = pl.ds(b * 256, 256)
        row_loads.append(pltpu.make_async_copy(rows_hbm.at[rows, :], rows_ref.at[rows, :], row_sems.at[b]))
    for load in (loads[0], row_loads[0], loads[1], *row_loads[1:], loads[2]):
        load.start()
    unfold = unfold_matrix()
    copies = []
    for b in range(4):
        rows = slice(b * 256, (b + 1) * 256)
        if b == 0:
            loads[0].wait()
        row_loads[b].wait()
        piece = dot(unfold, rows_ref[rows, half:]).astype(BF)
        for r in range(8):
            last_ref[r, b * 32 : (b + 1) * 32, :] = piece[r * 32 : (r + 1) * 32]
        if b == 3:
            loads[1].wait()
            loads[2].wait()
        for c in range(parts):
            cols = slice(c * FOLD, (c + 1) * FOLD)
            both = dot(gates_ref[:, rows], rows_ref[rows, cols])
            both = both[: 2 * tokens] + both[2 * tokens :]
            if b == 0:
                part_ref[:, cols] = both
            elif b < 3:
                part_ref[:, cols] += both
            else:
                both += part_ref[:, cols]
                for h in range(2):
                    at = h * half + c * FOLD
                    more = dot(ninth_ref[...], last_ref[h * parts + c])
                    out_ref[:, at : at + FOLD] = (
                        sum_ref[:, at : at + FOLD] + both[h * tokens : (h + 1) * tokens] + more[:tokens] + more[tokens:]
                    ).astype(BF)
                    columns = pl.ds(at, FOLD)
                    copies.append(
                        pltpu.make_async_copy(out_ref.at[:, columns], out_hbm.at[:, columns], out_sems.at[c, h])
                    )
                    copies[-1].start()
    for copy in copies:
        copy.wait()


def last_combine(gates, ninth, total, returned):
    rows = returned.shape[0]
    tokens, width = total.shape
    return pl.pallas_call(
        last_combine_kernel,
        in_specs=[pl.BlockSpec(memory_space=pl.ANY)] * 4,
        out_specs=pl.BlockSpec(memory_space=pl.ANY),
        out_shape=jax.ShapeDtypeStruct((tokens, width), BF),
        scratch_shapes=[
            pltpu.VMEM(gates.shape, BF),
            pltpu.VMEM(ninth.shape, BF),
            pltpu.VMEM(total.shape, F32),
            pltpu.VMEM(returned.shape, BF),
            pltpu.VMEM((8, 128, FOLD), BF),
            pltpu.VMEM((2 * tokens, width // 2), F32),
            pltpu.VMEM((tokens, width), BF),
            pltpu.SemaphoreType.DMA((rows // 256,)),
            pltpu.SemaphoreType.DMA((3,)),
            pltpu.SemaphoreType.DMA((width // 2 // FOLD, 2)),
        ],
        compiler_params=pltpu.CompilerParams(vmem_limit_bytes=VMEM),
        cost_estimate=pl.CostEstimate(flops=2 * 512 * 1152 * 2048, bytes_accessed=10_000_000, transcendentals=0),
        name="last_combine",
    )(gates, ninth, total, returned)


def attention_kernel(place_ref, queries_ref, *refs):
    *halves, out_ref = refs
    rows = queries_ref.shape[0]
    heads = queries_ref.shape[1] // HEAD_SIZE
    ahead = iota((rows, rows), 1) - iota((rows, rows), 0)
    blocks = halves[0].shape[0] // rows
    seen = [
        jnp.concatenate(
            [ahead <= (place_ref[0] - place_ref[i * blocks + j]) * rows for j in range(blocks)], axis=1
        )
        for i in range(2)
    ]
    factor = HEAD_SIZE**-0.5 * 1.4426950408889634
    for h in range(heads):
        cols = slice(h * HEAD_SIZE, (h + 1) * HEAD_SIZE)
        scores = []
        for i in range(2):
            raw = lax.dot_general(
                queries_ref[:, cols], halves[2 * i][...], (((1,), (1,)), ((), ())), preferred_element_type=F32
            )
            scores.append(jnp.where(seen[i], raw, -1e30))
        top = jnp.maximum(*(jnp.max(part, axis=-1, keepdims=True) for part in scores))
        parts = [jnp.exp2((part - top) * factor) for part in scores]
        total = sum(jnp.sum(part, axis=-1, keepdims=True) for part in parts)
        mixed = sum(dot(parts[i].astype(BF), halves[2 * i + 1][...]) for i in range(2))
        out_ref[:, cols] = (mixed / total).astype(BF)


def attention(places, queries, column, other, heads_per_step=16):
    rows, width = queries.shape
    length = column.shape[0]
    kv_heads = column.shape[1] // (2 * HEAD_SIZE)
    steps = width // (heads_per_step * HEAD_SIZE)
    per_kv = steps // kv_heads
    block = (rows, heads_per_step * HEAD_SIZE)
    keys = pl.BlockSpec((length, HEAD_SIZE), lambda i: (0, i // per_kv))
    values = pl.BlockSpec((length, HEAD_SIZE), lambda i: (0, kv_heads + i // per_kv))
    return pl.pallas_call(
        attention_kernel,
        grid=(steps,),
        in_specs=[
            pl.BlockSpec(memory_space=pltpu.SMEM),
            pl.BlockSpec(block, lambda i: (0, i)),
            keys,
            values,
            keys,
            values,
        ],
        out_specs=pl.BlockSpec(block, lambda i: (0, i)),
        out_shape=jax.ShapeDtypeStruct(queries.shape, BF),
        compiler_params=pltpu.CompilerParams(vmem_limit_bytes=VMEM),
        cost_estimate=pl.CostEstimate(
            flops=8 * rows * width * length,
            bytes_accessed=9_000_000,
            transcendentals=2 * rows * length * width // HEAD_SIZE,
        ),
        name="attention_rows",
    )(places, queries, column, column, other, other)


def at(y, z, core):
    return y * 8 + (z % 4) * 2 + core


def moved(rows, dy=0, dz=0, dcore=0):
    pairs = [
        (at(y, z, core), at((y + dy) % 2, z + dz, (core + dcore) % 2))
        for y in range(2) for z in range(4) for core in range(2)
    ]
    return lax.ppermute(rows, "seq", pairs)


def exchange(rows):
    return lax.all_to_all(rows, ("seq", "exp"), split_axis=0, concat_axis=0, tiled=True)


def on_device(queries, keys, values, tokens, routed, gates, up, down):
    tied = lax.optimization_barrier
    block = keys.shape[1]
    routed, gates = routed.T, gates.T
    pairs = jnp.concatenate([keys[0], values[0]], axis=1)
    across = moved(pairs, dy=1)
    outgoing = dispatch(routed, tokens, False)

    outgoing, pairs, across, routed, tokens, gates = tied((outgoing, pairs, across, routed, tokens, gates))
    arrived_1 = exchange(outgoing)
    outgoing = dispatch(routed, tokens, True)
    here = jnp.concatenate([pairs, across], axis=0)
    below, above = moved(here, dz=1), moved(here, dz=-1)
    weights_1, weights_2, weights_3 = gate_matrices(routed, gates)

    arrived_1, outgoing, here, below, above, weights_1, weights_2, weights_3 = tied(
        (arrived_1, outgoing, here, below, above, weights_1, weights_2, weights_3)
    )
    arrived_2 = exchange(outgoing)
    made = run_experts(arrived_1, up, down)
    far = [moved(below[:block], dz=1), moved(above[block:], dz=-1)]

    arrived_2, made, here, below, above, far = tied((arrived_2, made, here, below, above, far))
    returned_1 = exchange(made)
    made = run_experts(arrived_2, up, down)
    column = jnp.concatenate([here, below, above, *far], axis=0)
    other = moved(column, dcore=1)

    returned_1, made, column, other, own = tied((returned_1, made, column, other, queries[0]))
    returned_2 = exchange(made)
    total = first_combine(weights_1, returned_1)
    index = lax.axis_index("seq")
    y, z, core = index // 8, index // 2 % 4, index % 2
    places = [
        at((y + dy) % 2, z + dz, (core + dcore) % 2) for dcore in range(2) for dz in (0, -1, 1, 2) for dy in range(2)
    ]
    attended = attention(jnp.stack(places).astype(jnp.int32), own, column, other)
    return (attended[None], last_combine(weights_2, weights_3, total, returned_2))


def solution(mesh):
    spread = P(("seq", "exp"), None)
    in_specs = (P("exp", "seq", None),) * 3 + (spread,) * 3 + (P(("seq", "exp"), None, None),) * 2
    out_specs = (P("exp", "seq", None), spread)
    return jax.shard_map(on_device, mesh=mesh, in_specs=in_specs, out_specs=out_specs, check_vma=False)
```

```python
import functools

import jax
import jax.numpy as jnp
from jax import lax
from jax.experimental import pallas as pl
from jax.experimental.pallas import tpu as pltpu
from jax.sharding import PartitionSpec as P

HEAD_SIZE = 128
HALF = 4
LAST = 8
FOLD = 512
BF = jnp.bfloat16
F32 = jnp.float32
VMEM = 56 * 1024 * 1024


def iota(shape, dim):
    return lax.broadcasted_iota(jnp.int32, shape, dim)


def dot(a, b):
    return jnp.dot(a, b, preferred_element_type=F32)


def permutation(source):
    row, col = iota((256, 256), 0), iota((256, 256), 1)
    return (col == source(row)).astype(F32).astype(BF)


def fold_matrix():
    return permutation(lambda i: (i & 7) * 32 + (i >> 3))


def unfold_matrix():
    return permutation(lambda i: (i & 31) * 8 + (i >> 5))


def fold_half_matrix():
    return permutation(lambda i: ((i >> 2) & 1) * 128 + (i >> 3) * 4 + (i & 3))


def unfold_half_matrix():
    return permutation(lambda i: ((i >> 2) & 31) * 8 + (i >> 7) * 4 + (i & 3))


def ranks(routed):
    tokens = routed.shape[1]
    experts = iota((128, tokens), 0)
    named = jnp.zeros((128, tokens), F32)
    for j in range(routed.shape[0]):
        named = jnp.where(routed[j : j + 1, :] == experts, 1.0, named)
    earlier = (iota((tokens, tokens), 0) < iota((tokens, tokens), 1)).astype(F32).astype(BF)
    before = dot(named.astype(BF), earlier)
    return jnp.where(named > 0.5, before, -1.0)


def block_copy(source, target, b, columns, sem):
    rows = pl.ds(b * 256, 256)
    return pltpu.make_async_copy(source.at[rows, :], target.at[rows, columns], sem)


def dispatch_kernel(*refs, first, ninth):
    inputs = 2 if ninth else 4
    routed_hbm, tokens_hbm, *pair_inputs = refs[:inputs]
    out_hbm, *pair_output = refs[inputs : -9]
    routed_ref, tokens_ref, rows_ref, ninth_ref, fold_ref, pair_ref, in_sems, sems, pair_sems = refs[-9:]
    half = tokens_ref.shape[1]
    parts = half // FOLD
    loads = [
        pltpu.make_async_copy(
            tokens_hbm.at[:, pl.ds(h * half, half)], tokens_ref.at[pl.ds(h * 128, 128), :], in_sems.at[h]
        )
        for h in range(2)
    ]
    named = pltpu.make_async_copy(routed_hbm, routed_ref, in_sems.at[2])
    for load in (named, *loads):
        load.start()
    pair_loads = []
    for i, source in enumerate(pair_inputs):
        size = source.shape[1]
        pair_loads.append(pltpu.make_async_copy(source, pair_ref.at[:, pl.ds(i * size, size)], pair_sems.at[i]))
        pair_loads[-1].start()
    copies = []
    named.wait()
    rank = ranks(routed_ref[...])
    low = rank.astype(BF)
    row = iota((256, 128), 0)
    slot = ((row & 3) + first).astype(F32)
    upper = ((row >> 2) & 1) == 1
    for b in range(4):
        expand = (iota((256, 128), 1) == b * 32 + (row >> 3)).astype(F32).astype(BF)
        band = jnp.where(dot(expand, low) == slot, 1.0, 0.0)
        pick = jnp.concatenate([jnp.where(upper, 0.0, band), jnp.where(upper, band, 0.0)], axis=1).astype(BF)
        if b == 0:
            for load in loads:
                load.wait()
        for c in range(parts):
            cols = slice(c * FOLD, (c + 1) * FOLD)
            rows_ref[b * 256 : (b + 1) * 256, cols] = dot(pick, tokens_ref[:, cols]).astype(BF)
        copies.append(block_copy(rows_ref, out_hbm, b, pl.ds(0, half), sems.at[b, 0]))
        copies[-1].start()
        if pair_loads and b == 0:
            for load in pair_loads:
                load.wait()
            copies.append(pltpu.make_async_copy(pair_ref, pair_output[0], pair_sems.at[2]))
            copies[-1].start()
    if ninth:
        pick = jnp.where(rank == float(LAST), 1.0, 0.0).astype(BF)
        for r in range(2 * parts):
            h, c = divmod(r, parts)
            ninth_ref[r] = dot(pick, tokens_ref[h * 128 : (h + 1) * 128, c * FOLD : (c + 1) * FOLD]).astype(BF)
        fold = fold_matrix()
        for b in range(4):
            piece = jnp.concatenate([ninth_ref[r, b * 32 : (b + 1) * 32, :] for r in range(8)], axis=0)
            fold_ref[b * 256 : (b + 1) * 256, :] = dot(fold, piece).astype(BF)
            copies.append(block_copy(fold_ref, out_hbm, b, pl.ds(half, FOLD), sems.at[b, 1]))
            copies[-1].start()
    for copy in copies:
        copy.wait()


def dispatch(routed, tokens, pairs=()):
    second = not pairs
    half = tokens.shape[1] // 2
    shapes = [jax.ShapeDtypeStruct((1024, half + FOLD * second), BF)]
    if pairs:
        shapes.append(jax.ShapeDtypeStruct((pairs[0].shape[0], 2 * pairs[0].shape[1]), BF))
    return pl.pallas_call(
        functools.partial(dispatch_kernel, first=HALF * second, ninth=second),
        in_specs=[pl.BlockSpec(memory_space=pl.ANY)] * (2 + len(pairs)),
        out_specs=[pl.BlockSpec(memory_space=pl.ANY)] * len(shapes),
        out_shape=shapes,
        scratch_shapes=[
            pltpu.VMEM(routed.shape, jnp.int32),
            pltpu.VMEM((256, half), BF),
            pltpu.VMEM((1024, half), BF),
            pltpu.VMEM((8, 128, FOLD), BF),
            pltpu.VMEM((1024, FOLD), BF),
            pltpu.VMEM((128, 2 * FOLD), BF),
            pltpu.SemaphoreType.DMA((3,)),
            pltpu.SemaphoreType.DMA((4, 2)),
            pltpu.SemaphoreType.DMA((3,)),
        ],
        compiler_params=pltpu.CompilerParams(vmem_limit_bytes=VMEM),
        cost_estimate=pl.CostEstimate(flops=2 * 640 * 128 * 4096, bytes_accessed=6_000_000, transcendentals=0),
        name="dispatch_rows",
    )(routed, tokens, *pairs)


def gates_kernel(routed_ref, gates_ref, first_ref, second_ref, ninth_ref):
    routed = routed_ref[...]
    tokens = routed.shape[1]
    rank = ranks(routed)
    experts = iota((128, tokens), 0)
    gate = jnp.zeros((128, tokens), F32)
    for j in range(routed.shape[0]):
        gate = jnp.where(routed[j : j + 1, :] == experts, gates_ref[j : j + 1, :], gate)
    gate = gate.T
    rank = rank.T
    high = gate.astype(BF)
    low = (gate - high.astype(F32)).astype(BF)
    expand = (iota((128, 1024), 0) == (iota((128, 1024), 1) >> 3)).astype(F32).astype(BF)
    spread = dot(rank.astype(BF), expand)
    lane = iota((tokens, 1024), 1)
    slot = (lane & 3).astype(F32)
    for part, value in enumerate((high, low)):
        wide = dot(value, expand)
        ninth_ref[part * tokens : (part + 1) * tokens, :] = jnp.where(
            rank == float(LAST), value.astype(F32), 0.0
        ).astype(BF)
        for h in range(2):
            rows = slice((part * 2 + h) * tokens, (part * 2 + h + 1) * tokens)
            kept = jnp.where(((lane >> 2) & 1) == h, wide, 0.0)
            first_ref[rows, :] = jnp.where(spread == slot, kept, 0.0).astype(BF)
            second_ref[rows, :] = jnp.where(spread == slot + float(HALF), kept, 0.0).astype(BF)


def gate_matrices(routed, gates):
    tokens = routed.shape[1]
    shape = jax.ShapeDtypeStruct((4 * tokens, 1024), BF)
    return pl.pallas_call(
        gates_kernel,
        out_shape=(shape, shape, jax.ShapeDtypeStruct((2 * tokens, 128), BF)),
        compiler_params=pltpu.CompilerParams(vmem_limit_bytes=VMEM),
        cost_estimate=pl.CostEstimate(flops=200_000_000_000, bytes_accessed=2_200_000, transcendentals=0),
        name="gate_matrices",
    )(routed, gates)


def experts_kernel(
    rows_hbm, up_hbm, down_hbm, out_hbm,
    stage_ref, last_ref, rows_ref, up_ref, down_ref, hidden_ref, made_ref, sent_ref, fold_ref,
    row_sems, up_sems, down_sems, sems,
    *, ninth, part,
):
    half = stage_ref.shape[1]
    width = rows_ref.shape[1]
    units = hidden_ref.shape[1]
    count = rows_ref.shape[0] // 4
    parts = half // FOLD
    chunks = up_sems.shape[0]
    deep = width // chunks

    row_loads = []
    for b in range(4):
        rows = pl.ds(b * 256, 256)
        loads = [pltpu.make_async_copy(rows_hbm.at[rows, pl.ds(0, half)], stage_ref.at[rows, :], row_sems.at[b, 0])]
        if ninth:
            loads.append(
                pltpu.make_async_copy(rows_hbm.at[rows, pl.ds(half, FOLD)], last_ref.at[rows, :], row_sems.at[b, 1])
            )
        row_loads.append(loads)
    up_loads = [
        pltpu.make_async_copy(
            up_hbm.at[0, pl.ds(k * deep, deep), :], up_ref.at[pl.ds(k * deep, deep), :], up_sems.at[k]
        )
        for k in range(chunks)
    ]
    down_load = pltpu.make_async_copy(down_hbm.at[0], down_ref, down_sems.at[0])
    for loads in row_loads:
        for load in loads:
            load.start()
    for load in up_loads:
        load.start()
    down_load.start()

    unfold_half = unfold_half_matrix()
    for b in range(4):
        for load in row_loads[b]:
            load.wait()
        for c in range(parts):
            cols = slice(c * FOLD, (c + 1) * FOLD)
            both = dot(unfold_half, stage_ref[b * 256 : (b + 1) * 256, cols]).astype(BF)
            rows_ref[b * count : b * count + 128, cols] = both[:128]
            rows_ref[b * count : b * count + 128, half + c * FOLD : half + (c + 1) * FOLD] = both[128:]
        if ninth:
            piece = dot(unfold_matrix(), last_ref[b * 256 : (b + 1) * 256, :]).astype(BF)
            for r in range(8):
                rows_ref[b * count + 128 : (b + 1) * count, r * FOLD : (r + 1) * FOLD] = piece[r * 32 : (r + 1) * 32]
    for load in up_loads:
        load.wait()
    for c in range(units // part):
        cols = slice(c * part, (c + 1) * part)
        gate = dot(rows_ref[...], up_ref[:, cols])
        linear = dot(rows_ref[...], up_ref[:, units + c * part : units + (c + 1) * part])
        hidden_ref[:, cols] = (gate / (1.0 + jnp.exp(-gate)) * linear).astype(BF)
    down_load.wait()
    for c in range(width // FOLD):
        cols = slice(c * FOLD, (c + 1) * FOLD)
        made_ref[:, cols] = dot(hidden_ref[...], down_ref[:, cols]).astype(BF)
    copies = []
    fold_half = fold_half_matrix()
    for b in range(4):
        rows = slice(b * count, b * count + 128)
        for c in range(parts):
            cols = slice(c * FOLD, (c + 1) * FOLD)
            piece = jnp.concatenate(
                [made_ref[rows, cols], made_ref[rows, half + c * FOLD : half + (c + 1) * FOLD]], axis=0
            )
            sent_ref[b * 256 : (b + 1) * 256, cols] = dot(fold_half, piece).astype(BF)
        copies.append(block_copy(sent_ref, out_hbm, b, pl.ds(0, half), sems.at[b, 0]))
        copies[-1].start()
        if ninth:
            rows = slice(b * count + 128, (b + 1) * count)
            piece = jnp.concatenate([made_ref[rows, r * FOLD : (r + 1) * FOLD] for r in range(8)], axis=0)
            fold_ref[b * 256 : (b + 1) * 256, :] = dot(fold_matrix(), piece).astype(BF)
            copies.append(block_copy(fold_ref, out_hbm, b, pl.ds(half, FOLD), sems.at[b, 1]))
            copies[-1].start()
    for copy in copies:
        copy.wait()


def run_experts(arrived, up, down, part=256, chunks=4):
    width = up.shape[1]
    units = down.shape[1]
    half = width // 2
    ninth = arrived.shape[1] > half
    all_rows = 4 * (160 if ninth else 128)
    return pl.pallas_call(
        functools.partial(experts_kernel, ninth=ninth, part=part),
        in_specs=[pl.BlockSpec(memory_space=pl.ANY)] * 3,
        out_specs=pl.BlockSpec(memory_space=pl.ANY),
        out_shape=jax.ShapeDtypeStruct(arrived.shape, BF),
        scratch_shapes=[
            pltpu.VMEM((1024, half), BF),
            pltpu.VMEM((1024, FOLD), BF),
            pltpu.VMEM((all_rows, width), BF),
            pltpu.VMEM((width, 2 * units), BF),
            pltpu.VMEM((units, width), BF),
            pltpu.VMEM((all_rows, units), BF),
            pltpu.VMEM((all_rows, width), BF),
            pltpu.VMEM((1024, half), BF),
            pltpu.VMEM((1024, FOLD), BF),
            pltpu.SemaphoreType.DMA((4, 2)),
            pltpu.SemaphoreType.DMA((chunks,)),
            pltpu.SemaphoreType.DMA((1,)),
            pltpu.SemaphoreType.DMA((4, 2)),
        ],
        compiler_params=pltpu.CompilerParams(vmem_limit_bytes=VMEM),
        cost_estimate=pl.CostEstimate(
            flops=2 * all_rows * units * 3 * width, bytes_accessed=29_000_000, transcendentals=all_rows * units
        ),
        name="run_experts",
    )(arrived, up, down)


def first_combine_kernel(gates_ref, rows_ref, out_ref):
    tokens, width = out_ref.shape
    half = width // 2
    for c in range(half // FOLD):
        both = dot(gates_ref[...], rows_ref[:, c * FOLD : (c + 1) * FOLD])
        for h in range(2):
            at = h * half + c * FOLD
            out_ref[:, at : at + FOLD] = (
                both[h * tokens : (h + 1) * tokens] + both[(2 + h) * tokens : (3 + h) * tokens]
            )


def first_combine(gates, returned):
    tokens = gates.shape[0] // 4
    return pl.pallas_call(
        first_combine_kernel,
        out_shape=jax.ShapeDtypeStruct((tokens, 2 * returned.shape[1]), F32),
        compiler_params=pltpu.CompilerParams(vmem_limit_bytes=VMEM),
        cost_estimate=pl.CostEstimate(flops=2 * 512 * 1024 * 2048, bytes_accessed=7_500_000, transcendentals=0),
        name="first_combine",
    )(gates, returned)


def last_combine_kernel(
    gates_hbm, ninth_hbm, sum_hbm, rows_hbm, out_hbm,
    gates_ref, ninth_ref, sum_ref, rows_ref, last_ref, part_ref, out_ref, row_sems, sems, out_sems,
):
    tokens, width = out_ref.shape
    half = width // 2
    parts = half // FOLD
    loads = [
        pltpu.make_async_copy(gates_hbm, gates_ref, sems.at[0]),
        pltpu.make_async_copy(ninth_hbm, ninth_ref, sems.at[1]),
        pltpu.make_async_copy(sum_hbm, sum_ref, sems.at[2]),
    ]
    row_loads = []
    for b in range(4):
        rows = pl.ds(b * 256, 256)
        row_loads.append(pltpu.make_async_copy(rows_hbm.at[rows, :], rows_ref.at[rows, :], row_sems.at[b]))
    for load in (loads[0], row_loads[0], loads[1], *row_loads[1:], loads[2]):
        load.start()
    unfold = unfold_matrix()
    copies = []
    for b in range(4):
        rows = slice(b * 256, (b + 1) * 256)
        if b == 0:
            loads[0].wait()
        row_loads[b].wait()
        piece = dot(unfold, rows_ref[rows, half:]).astype(BF)
        for r in range(8):
            last_ref[r, b * 32 : (b + 1) * 32, :] = piece[r * 32 : (r + 1) * 32]
        if b == 3:
            loads[1].wait()
            loads[2].wait()
        for c in range(parts):
            cols = slice(c * FOLD, (c + 1) * FOLD)
            both = dot(gates_ref[:, rows], rows_ref[rows, cols])
            both = both[: 2 * tokens] + both[2 * tokens :]
            if b == 0:
                part_ref[:, cols] = both
            elif b < 3:
                part_ref[:, cols] += both
            else:
                both += part_ref[:, cols]
                for h in range(2):
                    at = h * half + c * FOLD
                    more = dot(ninth_ref[...], last_ref[h * parts + c])
                    out_ref[:, at : at + FOLD] = (
                        sum_ref[:, at : at + FOLD] + both[h * tokens : (h + 1) * tokens] + more[:tokens] + more[tokens:]
                    ).astype(BF)
                    columns = pl.ds(at, FOLD)
                    copies.append(
                        pltpu.make_async_copy(out_ref.at[:, columns], out_hbm.at[:, columns], out_sems.at[c, h])
                    )
                    copies[-1].start()
    for copy in copies:
        copy.wait()


def last_combine(gates, ninth, total, returned):
    rows = returned.shape[0]
    tokens, width = total.shape
    return pl.pallas_call(
        last_combine_kernel,
        in_specs=[pl.BlockSpec(memory_space=pl.ANY)] * 4,
        out_specs=pl.BlockSpec(memory_space=pl.ANY),
        out_shape=jax.ShapeDtypeStruct((tokens, width), BF),
        scratch_shapes=[
            pltpu.VMEM(gates.shape, BF),
            pltpu.VMEM(ninth.shape, BF),
            pltpu.VMEM(total.shape, F32),
            pltpu.VMEM(returned.shape, BF),
            pltpu.VMEM((8, 128, FOLD), BF),
            pltpu.VMEM((2 * tokens, width // 2), F32),
            pltpu.VMEM((tokens, width), BF),
            pltpu.SemaphoreType.DMA((rows // 256,)),
            pltpu.SemaphoreType.DMA((3,)),
            pltpu.SemaphoreType.DMA((width // 2 // FOLD, 2)),
        ],
        compiler_params=pltpu.CompilerParams(vmem_limit_bytes=VMEM),
        cost_estimate=pl.CostEstimate(flops=2 * 512 * 1152 * 2048, bytes_accessed=10_000_000, transcendentals=0),
        name="last_combine",
    )(gates, ninth, total, returned)


def attention_kernel(place_ref, queries_ref, *refs):
    *halves, out_ref = refs
    rows = queries_ref.shape[0]
    heads = queries_ref.shape[1] // HEAD_SIZE
    ahead = iota((rows, rows), 1) - iota((rows, rows), 0)
    blocks = halves[0].shape[0] // rows
    seen = [
        jnp.concatenate(
            [ahead <= (place_ref[0] - place_ref[i * blocks + j]) * rows for j in range(blocks)], axis=1
        )
        for i in range(2)
    ]
    factor = HEAD_SIZE**-0.5 * 1.4426950408889634
    for h in range(heads):
        cols = slice(h * HEAD_SIZE, (h + 1) * HEAD_SIZE)
        scores = []
        for i in range(2):
            raw = lax.dot_general(
                queries_ref[:, cols], halves[2 * i][...], (((1,), (1,)), ((), ())), preferred_element_type=F32
            )
            scores.append(jnp.where(seen[i], raw, -1e30))
        top = jnp.maximum(*(jnp.max(part, axis=-1, keepdims=True) for part in scores))
        parts = [jnp.exp2((part - top) * factor) for part in scores]
        total = sum(jnp.sum(part, axis=-1, keepdims=True) for part in parts)
        mixed = sum(dot(parts[i].astype(BF), halves[2 * i + 1][...]) for i in range(2))
        out_ref[:, cols] = (mixed / total).astype(BF)


def attention(places, queries, column, other, heads_per_step=16):
    rows, width = queries.shape
    length = column.shape[0]
    kv_heads = column.shape[1] // (2 * HEAD_SIZE)
    steps = width // (heads_per_step * HEAD_SIZE)
    per_kv = steps // kv_heads
    block = (rows, heads_per_step * HEAD_SIZE)
    keys = pl.BlockSpec((length, HEAD_SIZE), lambda i: (0, i // per_kv))
    values = pl.BlockSpec((length, HEAD_SIZE), lambda i: (0, kv_heads + i // per_kv))
    return pl.pallas_call(
        attention_kernel,
        grid=(steps,),
        in_specs=[
            pl.BlockSpec(memory_space=pltpu.SMEM),
            pl.BlockSpec(block, lambda i: (0, i)),
            keys,
            values,
            keys,
            values,
        ],
        out_specs=pl.BlockSpec(block, lambda i: (0, i)),
        out_shape=jax.ShapeDtypeStruct(queries.shape, BF),
        compiler_params=pltpu.CompilerParams(vmem_limit_bytes=VMEM),
        cost_estimate=pl.CostEstimate(
            flops=8 * rows * width * length,
            bytes_accessed=9_000_000,
            transcendentals=2 * rows * length * width // HEAD_SIZE,
        ),
        name="attention_rows",
    )(places, queries, column, column, other, other)


def at(y, z, core):
    return y * 8 + (z % 4) * 2 + core


def moved(rows, dy=0, dz=0, dcore=0):
    pairs = [
        (at(y, z, core), at((y + dy) % 2, z + dz, (core + dcore) % 2))
        for y in range(2) for z in range(4) for core in range(2)
    ]
    return lax.ppermute(rows, "seq", pairs)


def exchange(rows):
    return lax.all_to_all(rows, ("seq", "exp"), split_axis=0, concat_axis=0, tiled=True)


def on_device(queries, keys, values, tokens, routed, gates, up, down):
    tied = lax.optimization_barrier
    block = keys.shape[1]
    routed, gates = routed.T, gates.T
    outgoing, pairs = dispatch(routed, tokens, (keys[0], values[0]))

    outgoing, pairs, routed, tokens, gates = tied((outgoing, pairs, routed, tokens, gates))
    arrived_1 = exchange(outgoing)
    across = moved(pairs, dy=1)
    pairs, across, named, gates = tied((pairs, across, routed, gates))
    weights_1, weights_2, weights_3 = gate_matrices(named, gates)
    pairs, across, weights_1 = tied((pairs, across, weights_1))
    here = jnp.concatenate([pairs, across], axis=0)
    below, above = moved(here, dz=1), moved(here, dz=-1)
    (outgoing,) = dispatch(routed, tokens)

    arrived_1, outgoing, here, below, above, weights_1, weights_2, weights_3 = tied(
        (arrived_1, outgoing, here, below, above, weights_1, weights_2, weights_3)
    )
    arrived_2 = exchange(outgoing)
    made = run_experts(arrived_1, up, down)
    far = [moved(below[:block], dz=1), moved(above[block:], dz=-1)]

    arrived_2, made, here, below, above, far = tied((arrived_2, made, here, below, above, far))
    returned_1 = exchange(made)
    made = run_experts(arrived_2, up, down)
    column = jnp.concatenate([here, below, above, *far], axis=0)
    other = moved(column, dcore=1)

    returned_1, made, column, other, own = tied((returned_1, made, column, other, queries[0]))
    returned_2 = exchange(made)
    total = first_combine(weights_1, returned_1)
    index = lax.axis_index("seq")
    y, z, core = index // 8, index // 2 % 4, index % 2
    places = [
        at((y + dy) % 2, z + dz, (core + dcore) % 2) for dcore in range(2) for dz in (0, -1, 1, 2) for dy in range(2)
    ]
    attended = attention(jnp.stack(places).astype(jnp.int32), own, column, other)
    return (attended[None], last_combine(weights_2, weights_3, total, returned_2))


def solution(mesh):
    spread = P(("seq", "exp"), None)
    in_specs = (P("exp", "seq", None),) * 3 + (spread,) * 3 + (P(("seq", "exp"), None, None),) * 2
    out_specs = (P("exp", "seq", None), spread)
    return jax.shard_map(on_device, mesh=mesh, in_specs=in_specs, out_specs=out_specs, check_vma=False)
```

```python
import functools

import jax
import jax.numpy as jnp
from jax import lax
from jax.experimental import pallas as pl
from jax.experimental.pallas import tpu as pltpu
from jax.sharding import PartitionSpec as P

HEAD_SIZE = 128
HALF = 4
LAST = 8
FOLD = 512
BF = jnp.bfloat16
F32 = jnp.float32
VMEM = 56 * 1024 * 1024


def iota(shape, dim):
    return lax.broadcasted_iota(jnp.int32, shape, dim)


def dot(a, b):
    return jnp.dot(a, b, preferred_element_type=F32)


def permutation(source):
    row, col = iota((256, 256), 0), iota((256, 256), 1)
    return (col == source(row)).astype(F32).astype(BF)


def fold_matrix():
    return permutation(lambda i: (i & 7) * 32 + (i >> 3))


def unfold_matrix():
    return permutation(lambda i: (i & 31) * 8 + (i >> 5))


def fold_half_matrix():
    return permutation(lambda i: ((i >> 2) & 1) * 128 + (i >> 3) * 4 + (i & 3))


def unfold_half_matrix():
    return permutation(lambda i: ((i >> 2) & 31) * 8 + (i >> 7) * 4 + (i & 3))


def ranks(routed):
    tokens = routed.shape[1]
    experts = iota((128, tokens), 0)
    named = jnp.zeros((128, tokens), F32)
    for j in range(routed.shape[0]):
        named = jnp.where(routed[j : j + 1, :] == experts, 1.0, named)
    earlier = (iota((tokens, tokens), 0) < iota((tokens, tokens), 1)).astype(F32).astype(BF)
    before = dot(named.astype(BF), earlier)
    return jnp.where(named > 0.5, before, -1.0)


def block_copy(source, target, b, columns, sem):
    rows = pl.ds(b * 256, 256)
    return pltpu.make_async_copy(source.at[rows, :], target.at[rows, columns], sem)


def dispatch_kernel(*refs, first, ninth):
    inputs = 4 if ninth else 2
    routed_hbm, tokens_hbm, *pair_inputs = refs[:inputs]
    out_hbm, *pair_output = refs[inputs : -9]
    routed_ref, tokens_ref, rows_ref, ninth_ref, fold_ref, pair_ref, in_sems, sems, pair_sems = refs[-9:]
    half = tokens_ref.shape[1]
    parts = half // FOLD
    loads = [
        pltpu.make_async_copy(
            tokens_hbm.at[:, pl.ds(h * half, half)], tokens_ref.at[pl.ds(h * 128, 128), :], in_sems.at[h]
        )
        for h in range(2)
    ]
    named = pltpu.make_async_copy(routed_hbm, routed_ref, in_sems.at[2])
    for load in (named, *loads):
        load.start()
    pair_loads = []
    for i, source in enumerate(pair_inputs):
        size = source.shape[1]
        pair_loads.append(pltpu.make_async_copy(source, pair_ref.at[:, pl.ds(i * size, size)], pair_sems.at[i]))
        pair_loads[-1].start()
    copies = []
    named.wait()
    rank = ranks(routed_ref[...])
    low = rank.astype(BF)
    row = iota((256, 128), 0)
    slot = ((row & 3) + first).astype(F32)
    upper = ((row >> 2) & 1) == 1
    for b in range(4):
        expand = (iota((256, 128), 1) == b * 32 + (row >> 3)).astype(F32).astype(BF)
        band = jnp.where(dot(expand, low) == slot, 1.0, 0.0)
        pick = jnp.concatenate([jnp.where(upper, 0.0, band), jnp.where(upper, band, 0.0)], axis=1).astype(BF)
        if b == 0:
            for load in loads:
                load.wait()
        for c in range(parts):
            cols = slice(c * FOLD, (c + 1) * FOLD)
            rows_ref[b * 256 : (b + 1) * 256, cols] = dot(pick, tokens_ref[:, cols]).astype(BF)
        copies.append(block_copy(rows_ref, out_hbm, b, pl.ds(0, half), sems.at[b, 0]))
        copies[-1].start()
        if pair_loads and b == 0:
            for load in pair_loads:
                load.wait()
            copies.append(pltpu.make_async_copy(pair_ref, pair_output[0], pair_sems.at[2]))
            copies[-1].start()
    if ninth:
        pick = jnp.where(rank == float(LAST), 1.0, 0.0).astype(BF)
        for r in range(2 * parts):
            h, c = divmod(r, parts)
            ninth_ref[r] = dot(pick, tokens_ref[h * 128 : (h + 1) * 128, c * FOLD : (c + 1) * FOLD]).astype(BF)
        fold = fold_matrix()
        for b in range(4):
            piece = jnp.concatenate([ninth_ref[r, b * 32 : (b + 1) * 32, :] for r in range(8)], axis=0)
            fold_ref[b * 256 : (b + 1) * 256, :] = dot(fold, piece).astype(BF)
            copies.append(block_copy(fold_ref, out_hbm, b, pl.ds(half, FOLD), sems.at[b, 1]))
            copies[-1].start()
    for copy in copies:
        copy.wait()


def dispatch(routed, tokens, pairs=()):
    second = not pairs
    half = tokens.shape[1] // 2
    shapes = [jax.ShapeDtypeStruct((1024, half + FOLD * (not second)), BF)]
    if pairs:
        shapes.append(jax.ShapeDtypeStruct((pairs[0].shape[0], 2 * pairs[0].shape[1]), BF))
    return pl.pallas_call(
        functools.partial(dispatch_kernel, first=HALF * second, ninth=not second),
        in_specs=[pl.BlockSpec(memory_space=pl.ANY)] * (2 + len(pairs)),
        out_specs=[pl.BlockSpec(memory_space=pl.ANY)] * len(shapes),
        out_shape=shapes,
        scratch_shapes=[
            pltpu.VMEM(routed.shape, jnp.int32),
            pltpu.VMEM((256, half), BF),
            pltpu.VMEM((1024, half), BF),
            pltpu.VMEM((8, 128, FOLD), BF),
            pltpu.VMEM((1024, FOLD), BF),
            pltpu.VMEM((128, 2 * FOLD), BF),
            pltpu.SemaphoreType.DMA((3,)),
            pltpu.SemaphoreType.DMA((4, 2)),
            pltpu.SemaphoreType.DMA((3,)),
        ],
        compiler_params=pltpu.CompilerParams(vmem_limit_bytes=VMEM),
        cost_estimate=pl.CostEstimate(flops=2 * 640 * 128 * 4096, bytes_accessed=6_000_000, transcendentals=0),
        name="dispatch_rows",
    )(routed, tokens, *pairs)


def gates_kernel(routed_ref, gates_ref, first_ref, second_ref, ninth_ref):
    routed = routed_ref[...]
    tokens = routed.shape[1]
    rank = ranks(routed)
    experts = iota((128, tokens), 0)
    gate = jnp.zeros((128, tokens), F32)
    for j in range(routed.shape[0]):
        gate = jnp.where(routed[j : j + 1, :] == experts, gates_ref[j : j + 1, :], gate)
    gate = gate.T
    rank = rank.T
    high = gate.astype(BF)
    low = (gate - high.astype(F32)).astype(BF)
    expand = (iota((128, 1024), 0) == (iota((128, 1024), 1) >> 3)).astype(F32).astype(BF)
    spread = dot(rank.astype(BF), expand)
    lane = iota((tokens, 1024), 1)
    slot = (lane & 3).astype(F32)
    for part, value in enumerate((high, low)):
        wide = dot(value, expand)
        ninth_ref[part * tokens : (part + 1) * tokens, :] = jnp.where(
            rank == float(LAST), value.astype(F32), 0.0
        ).astype(BF)
        for h in range(2):
            rows = slice((part * 2 + h) * tokens, (part * 2 + h + 1) * tokens)
            kept = jnp.where(((lane >> 2) & 1) == h, wide, 0.0)
            first_ref[rows, :] = jnp.where(spread == slot, kept, 0.0).astype(BF)
            second_ref[rows, :] = jnp.where(spread == slot + float(HALF), kept, 0.0).astype(BF)


def gate_matrices(routed, gates):
    tokens = routed.shape[1]
    shape = jax.ShapeDtypeStruct((4 * tokens, 1024), BF)
    return pl.pallas_call(
        gates_kernel,
        out_shape=(shape, shape, jax.ShapeDtypeStruct((2 * tokens, 128), BF)),
        compiler_params=pltpu.CompilerParams(vmem_limit_bytes=VMEM),
        cost_estimate=pl.CostEstimate(flops=200_000_000_000, bytes_accessed=2_200_000, transcendentals=0),
        name="gate_matrices",
    )(routed, gates)


def experts_kernel(
    rows_hbm, up_hbm, down_hbm, out_hbm,
    stage_ref, last_ref, rows_ref, up_ref, down_ref, hidden_ref, made_ref, sent_ref, fold_ref,
    row_sems, up_sems, down_sems, sems,
    *, ninth, part,
):
    half = stage_ref.shape[1]
    width = rows_ref.shape[1]
    units = hidden_ref.shape[1]
    count = rows_ref.shape[0] // 4
    parts = half // FOLD
    chunks = up_sems.shape[0]
    deep = width // chunks

    row_loads = []
    for b in range(4):
        rows = pl.ds(b * 256, 256)
        loads = [pltpu.make_async_copy(rows_hbm.at[rows, pl.ds(0, half)], stage_ref.at[rows, :], row_sems.at[b, 0])]
        if ninth:
            loads.append(
                pltpu.make_async_copy(rows_hbm.at[rows, pl.ds(half, FOLD)], last_ref.at[rows, :], row_sems.at[b, 1])
            )
        row_loads.append(loads)
    up_loads = [
        pltpu.make_async_copy(
            up_hbm.at[0, pl.ds(k * deep, deep), :], up_ref.at[pl.ds(k * deep, deep), :], up_sems.at[k]
        )
        for k in range(chunks)
    ]
    down_load = pltpu.make_async_copy(down_hbm.at[0], down_ref, down_sems.at[0])
    for loads in row_loads:
        for load in loads:
            load.start()
    for load in up_loads:
        load.start()
    down_load.start()

    unfold_half = unfold_half_matrix()
    for b in range(4):
        for load in row_loads[b]:
            load.wait()
        for c in range(parts):
            cols = slice(c * FOLD, (c + 1) * FOLD)
            both = dot(unfold_half, stage_ref[b * 256 : (b + 1) * 256, cols]).astype(BF)
            rows_ref[b * count : b * count + 128, cols] = both[:128]
            rows_ref[b * count : b * count + 128, half + c * FOLD : half + (c + 1) * FOLD] = both[128:]
        if ninth:
            piece = dot(unfold_matrix(), last_ref[b * 256 : (b + 1) * 256, :]).astype(BF)
            for r in range(8):
                rows_ref[b * count + 128 : (b + 1) * count, r * FOLD : (r + 1) * FOLD] = piece[r * 32 : (r + 1) * 32]
    for load in up_loads:
        load.wait()
    for c in range(units // part):
        cols = slice(c * part, (c + 1) * part)
        gate = dot(rows_ref[...], up_ref[:, cols])
        linear = dot(rows_ref[...], up_ref[:, units + c * part : units + (c + 1) * part])
        hidden_ref[:, cols] = (gate / (1.0 + jnp.exp(-gate)) * linear).astype(BF)
    down_load.wait()
    for c in range(width // FOLD):
        cols = slice(c * FOLD, (c + 1) * FOLD)
        made_ref[:, cols] = dot(hidden_ref[...], down_ref[:, cols]).astype(BF)
    copies = []
    fold_half = fold_half_matrix()
    for b in range(4):
        rows = slice(b * count, b * count + 128)
        for c in range(parts):
            cols = slice(c * FOLD, (c + 1) * FOLD)
            piece = jnp.concatenate(
                [made_ref[rows, cols], made_ref[rows, half + c * FOLD : half + (c + 1) * FOLD]], axis=0
            )
            sent_ref[b * 256 : (b + 1) * 256, cols] = dot(fold_half, piece).astype(BF)
        copies.append(block_copy(sent_ref, out_hbm, b, pl.ds(0, half), sems.at[b, 0]))
        copies[-1].start()
        if ninth:
            rows = slice(b * count + 128, (b + 1) * count)
            piece = jnp.concatenate([made_ref[rows, r * FOLD : (r + 1) * FOLD] for r in range(8)], axis=0)
            fold_ref[b * 256 : (b + 1) * 256, :] = dot(fold_matrix(), piece).astype(BF)
            copies.append(block_copy(fold_ref, out_hbm, b, pl.ds(half, FOLD), sems.at[b, 1]))
            copies[-1].start()
    for copy in copies:
        copy.wait()


def run_experts(arrived, up, down, part=256, chunks=4):
    width = up.shape[1]
    units = down.shape[1]
    half = width // 2
    ninth = arrived.shape[1] > half
    all_rows = 4 * (160 if ninth else 128)
    return pl.pallas_call(
        functools.partial(experts_kernel, ninth=ninth, part=part),
        in_specs=[pl.BlockSpec(memory_space=pl.ANY)] * 3,
        out_specs=pl.BlockSpec(memory_space=pl.ANY),
        out_shape=jax.ShapeDtypeStruct(arrived.shape, BF),
        scratch_shapes=[
            pltpu.VMEM((1024, half), BF),
            pltpu.VMEM((1024, FOLD), BF),
            pltpu.VMEM((all_rows, width), BF),
            pltpu.VMEM((width, 2 * units), BF),
            pltpu.VMEM((units, width), BF),
            pltpu.VMEM((all_rows, units), BF),
            pltpu.VMEM((all_rows, width), BF),
            pltpu.VMEM((1024, half), BF),
            pltpu.VMEM((1024, FOLD), BF),
            pltpu.SemaphoreType.DMA((4, 2)),
            pltpu.SemaphoreType.DMA((chunks,)),
            pltpu.SemaphoreType.DMA((1,)),
            pltpu.SemaphoreType.DMA((4, 2)),
        ],
        compiler_params=pltpu.CompilerParams(vmem_limit_bytes=VMEM),
        cost_estimate=pl.CostEstimate(
            flops=2 * all_rows * units * 3 * width, bytes_accessed=29_000_000, transcendentals=all_rows * units
        ),
        name="run_experts",
    )(arrived, up, down)


def first_combine_kernel(gates_ref, ninth_ref, rows_ref, out_ref, last_ref):
    tokens, width = out_ref.shape
    half = width // 2
    parts = half // FOLD
    unfold = unfold_matrix()
    for b in range(4):
        piece = dot(unfold, rows_ref[b * 256 : (b + 1) * 256, half:]).astype(BF)
        for r in range(8):
            last_ref[r, b * 32 : (b + 1) * 32, :] = piece[r * 32 : (r + 1) * 32]
    for c in range(parts):
        both = dot(gates_ref[...], rows_ref[:, c * FOLD : (c + 1) * FOLD])
        for h in range(2):
            at = h * half + c * FOLD
            more = dot(ninth_ref[...], last_ref[h * parts + c])
            out_ref[:, at : at + FOLD] = (
                both[h * tokens : (h + 1) * tokens] + both[(2 + h) * tokens : (3 + h) * tokens]
                + more[:tokens] + more[tokens:]
            )


def first_combine(gates, ninth, returned):
    tokens = gates.shape[0] // 4
    return pl.pallas_call(
        first_combine_kernel,
        out_shape=jax.ShapeDtypeStruct((tokens, 2 * (returned.shape[1] - FOLD)), F32),
        scratch_shapes=[pltpu.VMEM((8, 128, FOLD), BF)],
        compiler_params=pltpu.CompilerParams(vmem_limit_bytes=VMEM),
        cost_estimate=pl.CostEstimate(flops=2 * 512 * 1152 * 2048, bytes_accessed=8_500_000, transcendentals=0),
        name="first_combine",
    )(gates, ninth, returned)


def last_combine_kernel(
    gates_hbm, sum_hbm, rows_hbm, out_hbm,
    gates_ref, sum_ref, rows_ref, part_ref, out_ref, row_sems, sems, out_sems,
):
    tokens, width = out_ref.shape
    half = width // 2
    parts = half // FOLD
    loads = [
        pltpu.make_async_copy(gates_hbm, gates_ref, sems.at[0]),
        pltpu.make_async_copy(sum_hbm, sum_ref, sems.at[1]),
    ]
    row_loads = []
    for b in range(4):
        rows = pl.ds(b * 256, 256)
        row_loads.append(pltpu.make_async_copy(rows_hbm.at[rows, :], rows_ref.at[rows, :], row_sems.at[b]))
    for load in (loads[0], *row_loads, loads[1]):
        load.start()
    copies = []
    for b in range(4):
        rows = slice(b * 256, (b + 1) * 256)
        if b == 0:
            loads[0].wait()
        row_loads[b].wait()
        if b == 3:
            loads[1].wait()
        for c in range(parts):
            cols = slice(c * FOLD, (c + 1) * FOLD)
            both = dot(gates_ref[:, rows], rows_ref[rows, cols])
            both = both[: 2 * tokens] + both[2 * tokens :]
            if b == 0:
                part_ref[:, cols] = both
            elif b < 3:
                part_ref[:, cols] += both
            else:
                both += part_ref[:, cols]
                for h in range(2):
                    at = h * half + c * FOLD
                    out_ref[:, at : at + FOLD] = (
                        sum_ref[:, at : at + FOLD] + both[h * tokens : (h + 1) * tokens]
                    ).astype(BF)
                    columns = pl.ds(at, FOLD)
                    copies.append(
                        pltpu.make_async_copy(out_ref.at[:, columns], out_hbm.at[:, columns], out_sems.at[c, h])
                    )
                    copies[-1].start()
    for copy in copies:
        copy.wait()


def last_combine(gates, total, returned):
    rows = returned.shape[0]
    tokens, width = total.shape
    return pl.pallas_call(
        last_combine_kernel,
        in_specs=[pl.BlockSpec(memory_space=pl.ANY)] * 3,
        out_specs=pl.BlockSpec(memory_space=pl.ANY),
        out_shape=jax.ShapeDtypeStruct((tokens, width), BF),
        scratch_shapes=[
            pltpu.VMEM(gates.shape, BF),
            pltpu.VMEM(total.shape, F32),
            pltpu.VMEM(returned.shape, BF),
            pltpu.VMEM((2 * tokens, width // 2), F32),
            pltpu.VMEM((tokens, width), BF),
            pltpu.SemaphoreType.DMA((rows // 256,)),
            pltpu.SemaphoreType.DMA((2,)),
            pltpu.SemaphoreType.DMA((width // 2 // FOLD, 2)),
        ],
        compiler_params=pltpu.CompilerParams(vmem_limit_bytes=VMEM),
        cost_estimate=pl.CostEstimate(flops=2 * 512 * 1152 * 2048, bytes_accessed=10_000_000, transcendentals=0),
        name="last_combine",
    )(gates, total, returned)


def attention_kernel(place_ref, queries_ref, *refs):
    *halves, out_ref = refs
    rows = queries_ref.shape[0]
    heads = queries_ref.shape[1] // HEAD_SIZE
    ahead = iota((rows, rows), 1) - iota((rows, rows), 0)
    blocks = halves[0].shape[0] // rows
    seen = [
        jnp.concatenate(
            [ahead <= (place_ref[0] - place_ref[i * blocks + j]) * rows for j in range(blocks)], axis=1
        )
        for i in range(2)
    ]
    factor = HEAD_SIZE**-0.5 * 1.4426950408889634
    for h in range(heads):
        cols = slice(h * HEAD_SIZE, (h + 1) * HEAD_SIZE)
        scores = []
        for i in range(2):
            raw = lax.dot_general(
                queries_ref[:, cols], halves[2 * i][...], (((1,), (1,)), ((), ())), preferred_element_type=F32
            )
            scores.append(jnp.where(seen[i], raw, -1e30))
        top = jnp.maximum(*(jnp.max(part, axis=-1, keepdims=True) for part in scores))
        parts = [jnp.exp2((part - top) * factor) for part in scores]
        total = sum(jnp.sum(part, axis=-1, keepdims=True) for part in parts)
        mixed = sum(dot(parts[i].astype(BF), halves[2 * i + 1][...]) for i in range(2))
        out_ref[:, cols] = (mixed / total).astype(BF)


def attention(places, queries, column, other, heads_per_step=16):
    rows, width = queries.shape
    length = column.shape[0]
    kv_heads = column.shape[1] // (2 * HEAD_SIZE)
    steps = width // (heads_per_step * HEAD_SIZE)
    per_kv = steps // kv_heads
    block = (rows, heads_per_step * HEAD_SIZE)
    keys = pl.BlockSpec((length, HEAD_SIZE), lambda i: (0, i // per_kv))
    values = pl.BlockSpec((length, HEAD_SIZE), lambda i: (0, kv_heads + i // per_kv))
    return pl.pallas_call(
        attention_kernel,
        grid=(steps,),
        in_specs=[
            pl.BlockSpec(memory_space=pltpu.SMEM),
            pl.BlockSpec(block, lambda i: (0, i)),
            keys,
            values,
            keys,
            values,
        ],
        out_specs=pl.BlockSpec(block, lambda i: (0, i)),
        out_shape=jax.ShapeDtypeStruct(queries.shape, BF),
        compiler_params=pltpu.CompilerParams(vmem_limit_bytes=VMEM),
        cost_estimate=pl.CostEstimate(
            flops=8 * rows * width * length,
            bytes_accessed=9_000_000,
            transcendentals=2 * rows * length * width // HEAD_SIZE,
        ),
        name="attention_rows",
    )(places, queries, column, column, other, other)


def at(y, z, core):
    return y * 8 + (z % 4) * 2 + core


def moved(rows, dy=0, dz=0, dcore=0):
    pairs = [
        (at(y, z, core), at((y + dy) % 2, z + dz, (core + dcore) % 2))
        for y in range(2) for z in range(4) for core in range(2)
    ]
    return lax.ppermute(rows, "seq", pairs)


def exchange(rows):
    return lax.all_to_all(rows, ("seq", "exp"), split_axis=0, concat_axis=0, tiled=True)


def on_device(queries, keys, values, tokens, routed, gates, up, down):
    tied = lax.optimization_barrier
    block = keys.shape[1]
    routed, gates = routed.T, gates.T
    outgoing, pairs = dispatch(routed, tokens, (keys[0], values[0]))

    outgoing, pairs, routed, tokens, gates = tied((outgoing, pairs, routed, tokens, gates))
    arrived_1 = exchange(outgoing)
    across = moved(pairs, dy=1)
    pairs, across, named, gates = tied((pairs, across, routed, gates))
    weights_1, weights_2, weights_3 = gate_matrices(named, gates)
    pairs, across, weights_1 = tied((pairs, across, weights_1))
    here = jnp.concatenate([pairs, across], axis=0)
    below, above = moved(here, dz=1), moved(here, dz=-1)
    (outgoing,) = dispatch(routed, tokens)

    arrived_1, outgoing, here, below, above, weights_1, weights_2, weights_3 = tied(
        (arrived_1, outgoing, here, below, above, weights_1, weights_2, weights_3)
    )
    arrived_2 = exchange(outgoing)
    made = run_experts(arrived_1, up, down)
    far = [moved(below[:block], dz=1), moved(above[block:], dz=-1)]

    arrived_2, made, here, below, above, far = tied((arrived_2, made, here, below, above, far))
    returned_1 = exchange(made)
    made = run_experts(arrived_2, up, down)
    column = jnp.concatenate([here, below, above, *far], axis=0)
    other = moved(column, dcore=1)

    returned_1, made, column, other, own = tied((returned_1, made, column, other, queries[0]))
    returned_2 = exchange(made)
    total = first_combine(weights_1, weights_3, returned_1)
    index = lax.axis_index("seq")
    y, z, core = index // 8, index // 2 % 4, index % 2
    places = [
        at((y + dy) % 2, z + dz, (core + dcore) % 2) for dcore in range(2) for dz in (0, -1, 1, 2) for dy in range(2)
    ]
    attended = attention(jnp.stack(places).astype(jnp.int32), own, column, other)
    return (attended[None], last_combine(weights_2, total, returned_2))


def solution(mesh):
    spread = P(("seq", "exp"), None)
    in_specs = (P("exp", "seq", None),) * 3 + (spread,) * 3 + (P(("seq", "exp"), None, None),) * 2
    out_specs = (P("exp", "seq", None), spread)
    return jax.shard_map(on_device, mesh=mesh, in_specs=in_specs, out_specs=out_specs, check_vma=False)
```
